256 devices in a mesh: outer: 16 (over z, x_hi), lat: 4 (over y), lon: 4 (over x_lo, core).
Axes of the slice: x: 4 (x_hi: 2, x_lo: 2; x = x_hi * 2 + x_lo), y: 4, z: 8, core: 2. Of those that a mesh axis runs over, the one named last changes fastest.
Arguments:
- tokens: bfloat16 [384, 2, 48, 2048], P(('outer', 'lat'), None, 'lon'), may hold values from -6 to 6
- norm_gain: float32 [2048], replicated, may hold values from 0.4 to 1.6
- w_qkv: bfloat16 [2048, 3, 2048], P(None, None, 'outer'), may hold values from -20 to 20
- w_out: bfloat16 [2048, 2048], P('outer'), may hold values from -0.125 to 0.125
- grad_out: bfloat16 [384, 2, 48, 2048], P(('outer', 'lat'), None, 'lon'), may hold values from -6 to 6
Outputs:
- output: bfloat16 [384, 2, 48, 2048], P(('outer', 'lat'), None, 'lon')
- grad_tokens: bfloat16 [384, 2, 48, 2048], P(('outer', 'lat'), None, 'lon')
- grad_wqkv: float32 [2048, 3, 2048], P(None, None, 'outer')
- grad_wout: float32 [2048, 2048], P('outer')
- grad_gain: float32 [2048], replicated
The draws below stay inside these ranges and needn't reach their ends.
All inputs are finite; a program needn't handle non-finite values.
Results may differ from the reference program's by a relative error of at most 0.023.
Values may be sent and summed in bfloat16 or wider, within the bound.
No kernel may reach another device: no remote copies, remote signals or barrier semaphores. Data moves between devices by JAX's collectives and lax.ppermute only.
A program may use at most 128 MiB of HBM per device.

```python
import jax
import jax.numpy as jnp
from jax import lax

D = 2048
HEADS = 32
HEAD = 64
LEV = 2
CLAT = 3
WLON = 12
LAT = 384
LON = 48
N_OUTER = 16


def draw_w_qkv(key, part):
    key = jax.random.fold_in(key, 7)
    base = jnp.clip(jax.random.normal(key, (D, 3, D), jnp.float32), -4.0, 4.0) * D ** (-0.5)
    return base.astype(jnp.bfloat16)


def shard_levels(rng, shape, cuts, smallest, largest):
    def one(axis_at, blocks):
        heights = jax.random.uniform(jax.random.fold_in(jax.random.fold_in(rng, 6), axis_at), (blocks,), jnp.float32, smallest / len(cuts), largest / len(cuts))
        return jnp.repeat(jnp.exp(heights), shape[axis_at] // blocks).reshape((-1,) + (1,) * (len(shape) - axis_at - 1))

    loudness = one(*cuts[0])
    for cut in cuts[1:]:
        loudness = loudness * one(*cut)
    return loudness


def centred(rng, shape, scale, limit, shards=(), kind=jnp.bfloat16):
    result = scale * jax.random.normal(rng, shape, jnp.float32)
    if shards:
        result = result * shard_levels(rng, shape, shards, -0.22, 0.18)
    return jnp.clip(result, -limit, limit).astype(kind)


def setup_inputs(seed: int = 0) -> dict:
    arg_keys = jax.random.split(jax.random.key(seed), 6)
    return {
        "tokens": centred(arg_keys[0], (LAT, LEV, LON, D), 1.0, 6.0, ((0, 64), (2, 4))),
        "norm_gain": jnp.clip(1.0 + 0.12 * jax.random.normal(arg_keys[1], (D,), jnp.float32), 0.4, 1.6),
        "w_qkv": draw_w_qkv(jax.random.fold_in(arg_keys[5], 71), 0),
        "w_out": centred(arg_keys[3], (D, D), D ** -0.5, 0.125, ((0, 16),)),
        "grad_out": centred(arg_keys[4], (LAT, LEV, LON, D), 1.0, 6.0, ((0, 64), (2, 4))),
    }


epsilon = 1e-05

def normalize(tokens):
    values_f = tokens.astype(jnp.float32)
    average = lax.optimization_barrier(jnp.mean(values_f, -1, keepdims=True))
    centered = values_f - average
    inverse_std = lax.rsqrt(lax.optimization_barrier(jnp.mean(centered * centered, -1, keepdims=True)) + epsilon)
    return (centered * inverse_std, inverse_std)

def to_windows(tensor):
    latitude, levels, longitude, channels = tensor.shape
    shaped = tensor.reshape(latitude // (2 * CLAT), 2 * CLAT, levels, longitude // WLON, WLON, channels)
    shaped = shaped.transpose(0, 3, 1, 2, 4, 5)
    return shaped.reshape(-1, 2 * CLAT * levels * WLON, channels)

def from_windows(tensor, latitude, longitude):
    channels = tensor.shape[-1]
    shaped = tensor.reshape(latitude // (2 * CLAT), longitude // WLON, 2 * CLAT, LEV, WLON, channels)
    shaped = shaped.transpose(0, 2, 3, 1, 4, 5)
    return shaped.reshape(latitude, LEV, longitude, channels)

def reference(tokens, norm_gain, w_qkv, w_out, grad_out):
    latitude = tokens.shape[0]
    longitude = tokens.shape[2]
    offset = WLON // 2
    heads_dev = D // N_OUTER
    score_scale = HEAD ** (-0.5)
    standard, inverse_std = normalize(tokens)
    normed = (standard * norm_gain).astype(jnp.bfloat16)
    rolled = jnp.roll(normed, (-CLAT, -offset), axis=(0, 2))
    window_in = to_windows(rolled)
    window_count = window_in.shape[0]
    window_size = window_in.shape[1]
    lon_blocks = longitude // WLON
    lat_blocks = latitude // (2 * CLAT)
    wrapped = jnp.arange(window_count) >= (lat_blocks - 1) * lon_blocks
    half_index = jnp.arange(window_size) // (CLAT * LEV * WLON)
    same_half = half_index[:, None] == half_index[None, :]
    allowed = jnp.logical_or(jnp.logical_not(wrapped)[:, None, None], same_half[None])
    flat_in = window_in.reshape(-1, D)
    w_flat = w_qkv.reshape(D, 3 * D)
    projected = jnp.dot(flat_in, w_flat, preferred_element_type=jnp.float32).astype(jnp.bfloat16)
    projected = projected.reshape(window_count, window_size, 3, HEADS, HEAD).astype(jnp.float32)
    queries = projected[:, :, 0]
    keys_all = projected[:, :, 1]
    values = projected[:, :, 2]
    scores = jnp.einsum('nqhd,nkhd->nhqk', queries, keys_all) * score_scale
    scores = jnp.where(allowed[:, None], scores, -1e+30)
    softmax_weights = jax.nn.softmax(scores, axis=-1)
    weights_low = softmax_weights.astype(jnp.bfloat16).astype(jnp.float32)
    attended = jnp.einsum('nhqk,nkhd->nqhd', weights_low, values).astype(jnp.bfloat16).reshape(-1, D)
    branch = jnp.zeros((attended.shape[0], D), jnp.float32)
    for group_index in range(N_OUTER):
        lower = group_index * heads_dev
        partial_term = jnp.dot(attended[:, lower:lower + heads_dev], w_out[lower:lower + heads_dev], preferred_element_type=jnp.float32)
        branch = branch + lax.optimization_barrier(partial_term.astype(jnp.bfloat16)).astype(jnp.float32)
    branch_low = from_windows(branch.astype(jnp.bfloat16).reshape(window_count, window_size, D), latitude, longitude)
    branch_low = jnp.roll(branch_low, (CLAT, offset), axis=(0, 2))
    output = (tokens.astype(jnp.float32) + branch_low.astype(jnp.float32)).astype(jnp.bfloat16)
    cotangent = jnp.roll(grad_out, (-CLAT, -offset), axis=(0, 2))
    cot_flat = to_windows(cotangent).reshape(-1, D)
    grad_wout = jnp.dot(attended.T, cot_flat, preferred_element_type=jnp.float32)
    d_attended = jnp.dot(cot_flat, w_out.T, preferred_element_type=jnp.float32).astype(jnp.bfloat16)
    d_window = d_attended.reshape(window_count, window_size, HEADS, HEAD).astype(jnp.float32)
    d_weights = jnp.einsum('nqhd,nkhd->nhqk', d_window, values)
    row_dots = lax.optimization_barrier(jnp.sum(softmax_weights * d_weights, -1, keepdims=True))
    d_scores = (softmax_weights * (d_weights - row_dots) * score_scale).astype(jnp.bfloat16).astype(jnp.float32)
    d_query = jnp.einsum('nhqk,nkhd->nqhd', d_scores, keys_all)
    d_key = jnp.einsum('nhqk,nqhd->nkhd', d_scores, queries)
    d_value = jnp.einsum('nhqk,nqhd->nkhd', weights_low, d_window)
    d_projected = jnp.stack([d_query, d_key, d_value], axis=2).astype(jnp.bfloat16).reshape(-1, 3 * D)
    grad_wqkv = jnp.dot(flat_in.T, d_projected, preferred_element_type=jnp.float32).reshape(D, 3, D)
    d_three = d_projected.reshape(-1, 3, D)
    d_rolled = jnp.zeros((d_three.shape[0], D), jnp.float32)
    for group_index in range(N_OUTER):
        lower = group_index * heads_dev
        d_group = d_three[:, :, lower:lower + heads_dev].reshape(-1, 3 * heads_dev)
        w_group = w_qkv[:, :, lower:lower + heads_dev].reshape(D, 3 * heads_dev)
        partial_term = jnp.dot(d_group, w_group.T, preferred_element_type=jnp.float32)
        d_rolled = d_rolled + lax.optimization_barrier(partial_term.astype(jnp.bfloat16)).astype(jnp.float32)
    d_normed = from_windows(d_rolled.astype(jnp.bfloat16).reshape(window_count, window_size, D), latitude, longitude)
    d_normed = jnp.roll(d_normed, (CLAT, offset), axis=(0, 2)).astype(jnp.float32)
    grad_gain = lax.optimization_barrier(jnp.sum((d_normed * standard).reshape(-1, D), 0))
    scaled = d_normed * norm_gain
    d_local = inverse_std * (scaled - lax.optimization_barrier(jnp.mean(scaled, -1, keepdims=True)) - standard * lax.optimization_barrier(jnp.mean(scaled * standard, -1, keepdims=True)))
    grad_tokens = (grad_out.astype(jnp.float32) + d_local).astype(jnp.bfloat16)
    return (output, grad_tokens, grad_wqkv, grad_wout, grad_gain)
```

```python
import jax
import jax.numpy as jnp
from jax import lax
from jax.sharding import Mesh, PartitionSpec as P
from jax.experimental import pallas as pl
from jax.experimental.pallas import tpu as pltpu

D = 2048
HEAD = 64
LEV = 2
CLAT = 3
WLON = 12
WIN = 2 * CLAT * LEV * WLON
HALF = WIN // 2
SLOTS = 8
STEP = 2
ROWS = STEP * WIN
COLS = 256
HEADS_DEV = COLS // HEAD
SCALE = HEAD ** (-0.5)
BLK = 128
bf16 = jnp.bfloat16
f32 = jnp.float32


def nn(a, b):
    return lax.dot_general(a, b, (((1,), (0,)), ((), ())), preferred_element_type=f32)


def nt(a, b):
    return lax.dot_general(a, b, (((1,), (1,)), ((), ())), preferred_element_type=f32)


def tn(a, b):
    return lax.dot_general(a, b, (((0,), (0,)), ((), ())), preferred_element_type=f32)


def forward_kernel(cut_ref, x_ref, wg_ref, qkv_ref, att_ref, p_ref, own_ref, sib_ref, wq_ref, wo_ref):
    step = pl.program_id(0)

    @pl.when(step == 0)
    def _():
        for part in range(16):
            rows = slice(part * BLK, (part + 1) * BLK)
            for blk in range(2):
                for i in range(3):
                    wq_ref[rows, (2 * i + blk) * BLK : (2 * i + blk + 1) * BLK] = wg_ref[part, blk, i]
                wo_ref[blk * BLK : (blk + 1) * BLK, rows] = wg_ref[part, blk, 3]

    for n in range(3):
        cols = slice(n * COLS, (n + 1) * COLS)
        qkv_ref[:, cols] = nn(x_ref[...], wq_ref[:, cols]).astype(bf16)
    row = lax.broadcasted_iota(jnp.int32, (WIN, WIN), 0) >= HALF
    col = lax.broadcasted_iota(jnp.int32, (WIN, WIN), 1) >= HALF
    same = row == col
    for w in range(STEP):
        rows = slice(w * WIN, (w + 1) * WIN)
        allowed = jnp.logical_or(same, cut_ref[step * STEP + w] == 0)
        for h in range(HEADS_DEV):
            q = qkv_ref[rows, h * HEAD : (h + 1) * HEAD]
            k = qkv_ref[rows, COLS + h * HEAD : COLS + (h + 1) * HEAD]
            v = qkv_ref[rows, 2 * COLS + h * HEAD : 2 * COLS + (h + 1) * HEAD]
            s = jnp.where(allowed, nt(q, k) * SCALE, -1e30)
            e = jnp.exp(s - jnp.max(s, -1, keepdims=True))
            p = e / jnp.sum(e, -1, keepdims=True)
            p_ref[w, h] = p
            att_ref[rows, h * HEAD : (h + 1) * HEAD] = nn(p.astype(bf16), v).astype(bf16)

    def project(out_ref):
        for n in range(8):
            cols = slice(n * COLS, (n + 1) * COLS)
            out_ref[:, cols] = nn(att_ref[...], wo_ref[:, cols]).astype(bf16)

    @pl.when(step < SLOTS // STEP // 2)
    def _():
        project(own_ref)

    @pl.when(step >= SLOTS // STEP // 2)
    def _():
        project(sib_ref)


def backward_kernel(cot_ref, qkv_ref, p_ref, wq_ref, wo_ref, dp_ref, own_ref, sib_ref):
    step = pl.program_id(0)
    d_att = nt(cot_ref[...], wo_ref[...]).astype(bf16)
    for w in range(STEP):
        rows = slice(w * WIN, (w + 1) * WIN)
        for h in range(HEADS_DEV):
            hc = slice(h * HEAD, (h + 1) * HEAD)
            q = qkv_ref[rows, h * HEAD : (h + 1) * HEAD]
            k = qkv_ref[rows, COLS + h * HEAD : COLS + (h + 1) * HEAD]
            v = qkv_ref[rows, 2 * COLS + h * HEAD : 2 * COLS + (h + 1) * HEAD]
            p = p_ref[w, h]
            d_o = d_att[rows, hc]
            d_w = nt(d_o, v)
            dots = jnp.sum(p * d_w, -1, keepdims=True)
            d_s = (p * (d_w - dots) * SCALE).astype(bf16)
            dp_ref[rows, h * HEAD : (h + 1) * HEAD] = nn(d_s, k).astype(bf16)
            dp_ref[rows, COLS + h * HEAD : COLS + (h + 1) * HEAD] = tn(d_s, q).astype(bf16)
            dp_ref[rows, 2 * COLS + h * HEAD : 2 * COLS + (h + 1) * HEAD] = tn(p.astype(bf16), d_o).astype(bf16)

    def project(out_ref):
        for n in range(8):
            cols = slice(n * COLS, (n + 1) * COLS)
            out_ref[:, cols] = nt(dp_ref[...], wq_ref[cols, :]).astype(bf16)

    @pl.when(step < SLOTS // STEP // 2)
    def _():
        project(own_ref)

    @pl.when(step >= SLOTS // STEP // 2)
    def _():
        project(sib_ref)


def grads_kernel(x_ref, cot_ref, dp_ref, att_ref, g_ref):
    gq = tn(x_ref[...], dp_ref[...]).astype(bf16)
    go = tn(att_ref[...], cot_ref[...]).astype(bf16)
    for part in range(2):
        rows = slice(part * BLK, (part + 1) * BLK)
        for blk in range(2):
            for i in range(3):
                g_ref[part, blk, i] = gq[rows, (2 * i + blk) * BLK : (2 * i + blk + 1) * BLK]
            g_ref[part, blk, 3] = go[blk * BLK : (blk + 1) * BLK, rows]


def params():
    return pltpu.CompilerParams(dimension_semantics=("arbitrary",), vmem_limit_bytes=56 * 1024 * 1024)


HALF_STEPS = SLOTS // STEP // 2
own_spec = pl.BlockSpec((ROWS, D), lambda i: (jnp.minimum(i, HALF_STEPS - 1), 0))
sib_spec = pl.BlockSpec((ROWS, D), lambda i: (jnp.maximum(i - HALF_STEPS, 0), 0))


def rows_spec(cols):
    return pl.BlockSpec((ROWS, cols), lambda i: (i, 0))


def whole(*shape):
    return pl.BlockSpec(shape, lambda i: (0,) * len(shape))


def cost(flops, nbytes, exps=0):
    return pl.CostEstimate(flops=flops, bytes_accessed=nbytes, transcendentals=exps)


def shaped(shape, dtype=bf16):
    return jax.ShapeDtypeStruct(shape, dtype)


TOK = SLOTS * WIN


def forward(cut, x, wg):
    return pl.pallas_call(
        forward_kernel,
        grid=(SLOTS // STEP,),
        in_specs=[
            pl.BlockSpec(memory_space=pltpu.SMEM),
            rows_spec(D),
            whole(16, 2, 4, BLK, BLK),
        ],
        out_specs=[
            rows_spec(3 * COLS),
            rows_spec(COLS),
            pl.BlockSpec((STEP, HEADS_DEV, WIN, WIN), lambda i: (i, 0, 0, 0)),
            own_spec,
            sib_spec,
            whole(D, 3 * COLS),
            whole(COLS, D),
        ],
        out_shape=[
            shaped((TOK, 3 * COLS)),
            shaped((TOK, COLS)),
            shaped((SLOTS, HEADS_DEV, WIN, WIN), f32),
            shaped((TOK // 2, D)),
            shaped((TOK // 2, D)),
            shaped((D, 3 * COLS)),
            shaped((COLS, D)),
        ],
        compiler_params=params(),
        cost_estimate=cost(2 * TOK * D * 4 * COLS, 25 << 20, SLOTS * HEADS_DEV * WIN * WIN),
        name="attention_forward",
    )(cut, x, wg)


def backward(cot, qkv, p, wq, wo):
    return pl.pallas_call(
        backward_kernel,
        grid=(SLOTS // STEP,),
        in_specs=[
            rows_spec(D),
            rows_spec(3 * COLS),
            pl.BlockSpec((STEP, HEADS_DEV, WIN, WIN), lambda i: (i, 0, 0, 0)),
            whole(D, 3 * COLS),
            whole(COLS, D),
        ],
        out_specs=[rows_spec(3 * COLS), own_spec, sib_spec],
        out_shape=[shaped((TOK, 3 * COLS)), shaped((TOK // 2, D)), shaped((TOK // 2, D))],
        compiler_params=params(),
        cost_estimate=cost(2 * TOK * D * 4 * COLS, 25 << 20),
        name="attention_backward",
    )(cot, qkv, p, wq, wo)


def grads(x, cot, dp, att):
    return pl.pallas_call(
        grads_kernel,
        grid=(8,),
        in_specs=[
            pl.BlockSpec((TOK, 2 * BLK), lambda i: (0, i)),
            pl.BlockSpec((TOK, 2 * BLK), lambda i: (0, i)),
            whole(TOK, 3 * COLS),
            whole(TOK, COLS),
        ],
        out_specs=pl.BlockSpec((2, 2, 4, BLK, BLK), lambda i: (i, 0, 0, 0, 0)),
        out_shape=shaped((16, 2, 4, BLK, BLK)),
        compiler_params=params(),
        cost_estimate=cost(2 * TOK * D * 4 * COLS, 16 << 20),
        name="weight_gradients",
    )(x, cot, dp, att)


ALL = ("zh", "zl", "xh", "lat", "xl", "core")
OUTER = ("zh", "zl", "xh")
ROW = ("zh", "zl", "xh", "lat")
LON = ("xl", "core")
NEAR = ("zl", "xh")
PLANE = ("lat", "xl", "core")
EPSILON = 1e-05


def shift(x, axes, by):
    count = lax.axis_size(axes)
    return lax.ppermute(x, axes, [(i, (i + by) % count) for i in range(count)])


def swap(x, axes, mask):
    count = lax.axis_size(axes)
    return lax.ppermute(x, axes, [(i, i ^ mask) for i in range(count)])


def shift_both(x, by):
    rows, cols = lax.axis_size(ROW), lax.axis_size(LON)
    pairs = [
        (r * cols + c, (r + by) % rows * cols + (c + by) % cols)
        for r in range(rows)
        for c in range(cols)
    ]
    return lax.ppermute(x, ALL, pairs)


def roll_in(x):
    lon = WLON // 2
    corner = shift_both(x[:CLAT, :, :lon], -1)
    below = shift(x[:CLAT, :, lon:], ROW, -1)
    right = shift(x[CLAT:, :, :lon], LON, -1)
    top = jnp.concatenate([x[CLAT:, :, lon:], right], axis=2)
    bottom = jnp.concatenate([below, corner], axis=2)
    return jnp.concatenate([top, bottom], axis=0).reshape(WIN, D)


def roll_out(x):
    x = x.reshape(2 * CLAT, LEV, WLON, D)
    lon = WLON // 2
    corner = shift_both(x[CLAT:, :, lon:], 1)
    above = shift(x[CLAT:, :, :lon], ROW, 1)
    left = shift(x[:CLAT, :, lon:], LON, 1)
    top = jnp.concatenate([corner, above], axis=2)
    bottom = jnp.concatenate([left, x[:CLAT, :, :lon]], axis=2)
    return jnp.concatenate([top, bottom], axis=0)


def normalize(tokens):
    values = tokens.astype(f32)
    average = jnp.mean(values, -1, keepdims=True)
    centered = values - average
    inverse_std = lax.rsqrt(jnp.mean(centered * centered, -1, keepdims=True) + EPSILON)
    return centered * inverse_std, inverse_std


def share(x):
    mine = [x] + [swap(x, NEAR, s) for s in (1, 2, 3)]
    theirs = [swap(part, "core", 1) for part in mine]
    return jnp.concatenate(mine + theirs, axis=0)


def collect(own, sib):
    own = own.reshape(4, WIN, D)
    sib = sib.reshape(4, WIN, D)
    sums = {}
    for s in (3, 2, 1, 0):
        sums[s] = own[s].astype(f32) + swap(sib[s], "core", 1).astype(f32)
    total = sums[0]
    for s in (3, 2, 1):
        total = total + swap(sums[s].astype(bf16), NEAR, s).astype(f32)
    return total.astype(bf16)


def gather_weights(w_qkv, w_out):
    part = lax.axis_index(PLANE) * BLK
    qkv = lax.dynamic_slice(w_qkv, (part, 0, 0), (BLK, 3, BLK)).transpose(1, 0, 2)
    out = lax.dynamic_slice(w_out, (0, part), (BLK, BLK))
    unit = jnp.concatenate([qkv, out[None]], axis=0)
    blocks = lax.all_gather(unit, "zh", axis=0)
    mine = lax.all_to_all(blocks, "core", 0, 0, tiled=True)
    return lax.all_gather(mine.reshape(2, 2, 4, BLK, BLK), ("lat", "xl"), axis=0, tiled=True)


def reduce_weights(g):
    part = lax.psum_scatter(g, ("lat", "xl"), scatter_dimension=0, tiled=True)
    blocks = lax.all_to_all(part.reshape(4, 4, BLK, BLK), "core", 0, 0, tiled=True)
    unit = lax.psum_scatter(blocks, "zh", scatter_dimension=0, tiled=False)
    whole_block = lax.all_gather(unit, PLANE, axis=0)
    grad_qkv = whole_block[:, :3].transpose(0, 2, 1, 3).reshape(D, 3, BLK).astype(f32)
    grad_out = whole_block[:, 3].transpose(1, 0, 2).reshape(BLK, D).astype(f32)
    return grad_qkv, grad_out


def shards(tokens, norm_gain, w_qkv, w_out, grad_out):
    wg = gather_weights(w_qkv, w_out)
    rolled = roll_in(tokens)
    standard, inverse_std = normalize(rolled)
    normed = (standard * norm_gain).astype(bf16)
    x = share(normed)
    cotangent = roll_in(grad_out)
    cot = share(cotangent)

    near = lax.axis_index(NEAR)
    edge = jnp.logical_and(lax.axis_index("zh") == 3, lax.axis_index("lat") == 3)
    owners = near ^ (jnp.arange(SLOTS) % 4)
    cut = jnp.logical_and(edge, owners == 3).astype(jnp.int32)

    qkv, att, p, own, sib, wq, wo = forward(cut, x, wg)
    branch = collect(own, sib)
    output = roll_out((rolled.astype(f32) + branch.astype(f32)).astype(bf16))

    dp, d_own, d_sib = backward(cot, qkv, p, wq, wo)
    g = grads(x, cot, dp, att)
    grad_wqkv, grad_wout = reduce_weights(g)

    d_normed = collect(d_own, d_sib).astype(f32)
    gain_sum = jnp.sum(d_normed * standard, 0).reshape(16, BLK)
    for bit in range(8):
        gain_sum = gain_sum + swap(gain_sum, ALL, 1 << bit)
    scaled = d_normed * norm_gain
    d_local = inverse_std * (
        scaled
        - jnp.mean(scaled, -1, keepdims=True)
        - standard * jnp.mean(scaled * standard, -1, keepdims=True)
    )
    grad_tokens = roll_out((cotangent.astype(f32) + d_local).astype(bf16))
    return output, grad_tokens, grad_wqkv, grad_wout, gain_sum.reshape(D)


def solution(mesh):
    fine = Mesh(mesh.devices.reshape(4, 2, 2, 4, 2, 2), ALL)
    by_token = P(ROW, None, LON, None)
    in_specs = (by_token, P(), P(None, None, OUTER), P(OUTER, None), by_token)
    out_specs = (by_token, by_token, P(None, None, OUTER), P(OUTER, None), P())
    return jax.shard_map(shards, mesh=fine, in_specs=in_specs, out_specs=out_specs, check_vma=False)
```

```python
import jax
import jax.numpy as jnp
from jax import lax
from jax.experimental import pallas as pl
from jax.experimental.pallas import tpu as pltpu
from jax.sharding import Mesh, PartitionSpec as P

D = 2048
HEAD = 64
LEV = 2
CLAT = 3
WLON = 12
WIN = 2 * CLAT * LEV * WLON
HALF = WIN // 2
SLOTS = 8
STEP = 2
ROWS = STEP * WIN
TOK = SLOTS * WIN
COLS = 256
HEADS_DEV = COLS // HEAD
SCALE = HEAD ** (-0.5)
BLK = 128
EPSILON = 1e-05
bf16 = jnp.bfloat16
f32 = jnp.float32

ALL = ("zh", "zl", "xh", "lat", "xl", "core")
OUTER = ("zh", "zl", "xh")
ROW = ("zh", "zl", "xh", "lat")
LON = ("xl", "core")
NEAR = ("zl", "xh")


def nn(a, b):
    return lax.dot_general(a, b, (((1,), (0,)), ((), ())), preferred_element_type=f32)


def nt(a, b):
    return lax.dot_general(a, b, (((1,), (1,)), ((), ())), preferred_element_type=f32)


def tn(a, b):
    return lax.dot_general(a, b, (((0,), (0,)), ((), ())), preferred_element_type=f32)


def forward_kernel(cut_ref, pos_ref, x_ref, *refs):
    pieces, (qkv_ref, att_ref, p_ref, wq_ref, wo_ref) = refs[:8], refs[8:]
    step = pl.program_id(0)

    @pl.when(step == 0)
    def _():
        for n, piece in enumerate(pieces):
            for c in range(2):
                rows = pl.ds(pl.multiple_of(pos_ref[2 * n + c] * BLK, BLK), BLK)
                for blk in range(2):
                    for i in range(3):
                        wq_ref[rows, (2 * i + blk) * BLK : (2 * i + blk + 1) * BLK] = piece[c, blk, i]
                    wo_ref[rows, blk * BLK : (blk + 1) * BLK] = piece[c, blk, 3]

    for n in range(3):
        cols = slice(n * COLS, (n + 1) * COLS)
        qkv_ref[:, cols] = nn(x_ref[...], wq_ref[:, cols]).astype(bf16)
    row = lax.broadcasted_iota(jnp.int32, (WIN, WIN), 0) >= HALF
    col = lax.broadcasted_iota(jnp.int32, (WIN, WIN), 1) >= HALF
    same = row == col
    for w in range(STEP):
        rows = slice(w * WIN, (w + 1) * WIN)
        allowed = jnp.logical_or(same, cut_ref[step * STEP + w] == 0)
        for h in range(HEADS_DEV):
            q = qkv_ref[rows, h * HEAD : (h + 1) * HEAD]
            k = qkv_ref[rows, COLS + h * HEAD : COLS + (h + 1) * HEAD]
            v = qkv_ref[rows, 2 * COLS + h * HEAD : 2 * COLS + (h + 1) * HEAD]
            s = jnp.where(allowed, nt(q, k) * SCALE, -1e30)
            e = jnp.exp(s - jnp.max(s, -1, keepdims=True))
            p = e / jnp.sum(e, -1, keepdims=True)
            p_ref[w, h] = p
            att_ref[rows, h * HEAD : (h + 1) * HEAD] = nn(p.astype(bf16), v).astype(bf16)


def backward_kernel(cot_ref, qkv_ref, p_ref, wo_ref, dp_ref):
    d_att = nn(cot_ref[...], wo_ref[...]).astype(bf16)
    for w in range(STEP):
        rows = slice(w * WIN, (w + 1) * WIN)
        for h in range(HEADS_DEV):
            q = qkv_ref[rows, h * HEAD : (h + 1) * HEAD]
            k = qkv_ref[rows, COLS + h * HEAD : COLS + (h + 1) * HEAD]
            v = qkv_ref[rows, 2 * COLS + h * HEAD : 2 * COLS + (h + 1) * HEAD]
            p = p_ref[w, h]
            d_o = d_att[rows, h * HEAD : (h + 1) * HEAD]
            d_w = nt(d_o, v)
            dots = jnp.sum(p * d_w, -1, keepdims=True)
            d_s = (p * (d_w - dots) * SCALE).astype(bf16)
            dp_ref[rows, h * HEAD : (h + 1) * HEAD] = nn(d_s, k).astype(bf16)
            dp_ref[rows, COLS + h * HEAD : COLS + (h + 1) * HEAD] = tn(d_s, q).astype(bf16)
            dp_ref[rows, 2 * COLS + h * HEAD : 2 * COLS + (h + 1) * HEAD] = tn(p.astype(bf16), d_o).astype(bf16)


def grads_kernel(where_ref, x_ref, cot_ref, dp_ref, att_ref, *g_refs):
    step = pl.program_id(0)
    core = where_ref[len(g_refs)]
    gq = tn(x_ref[...], dp_ref[...]).astype(bf16)
    go = tn(cot_ref[...], att_ref[...]).astype(bf16)
    for n, g_ref in enumerate(g_refs):

        @pl.when(step == n)
        def _():
            for part in range(2):
                rows = slice(part * BLK, (part + 1) * BLK)
                place = part ^ core
                for blk in range(2):
                    for i in range(3):
                        g_ref[place, blk, i] = gq[rows, (2 * i + blk) * BLK : (2 * i + blk + 1) * BLK]
                    g_ref[place, blk, 3] = go[rows, blk * BLK : (blk + 1) * BLK]


def project_kernel(a_ref, w_ref, own_ref, sib_ref):
    step = pl.program_id(0)

    def project(out_ref):
        for n in range(8):
            cols = slice(n * COLS, (n + 1) * COLS)
            out_ref[:, cols] = nt(a_ref[...], w_ref[cols, :]).astype(bf16)

    @pl.when(step < SLOTS // STEP // 2)
    def _():
        project(own_ref)

    @pl.when(step >= SLOTS // STEP // 2)
    def _():
        project(sib_ref)


def finish_kernel(where_ref, a_ref, b_ref, c_ref, d_ref, gq_ref, go_ref):
    for n, ref in enumerate((a_ref, b_ref, c_ref, d_ref)):
        rows = pl.ds(pl.multiple_of(where_ref[4 + n] * BLK, BLK), BLK)
        for i in range(3):
            gq_ref[i, rows, :] = ref[0, i].astype(f32)
        go_ref[:, rows] = ref[0, 3].astype(f32).T


def params():
    return pltpu.CompilerParams(dimension_semantics=("arbitrary",), vmem_limit_bytes=56 * 1024 * 1024)


HALF_STEPS = SLOTS // STEP // 2
own_spec = pl.BlockSpec((ROWS, D), lambda i: (jnp.minimum(i, HALF_STEPS - 1), 0))
sib_spec = pl.BlockSpec((ROWS, D), lambda i: (jnp.maximum(i - HALF_STEPS, 0), 0))
p_spec = pl.BlockSpec((STEP, HEADS_DEV, WIN, WIN), lambda i: (i, 0, 0, 0))
smem = pl.BlockSpec(memory_space=pltpu.SMEM)


def rows_spec(cols):
    return pl.BlockSpec((ROWS, cols), lambda i: (i, 0))


def whole(*shape):
    return pl.BlockSpec(shape, lambda *i: (0,) * len(shape))


def cost(flops, nbytes, exps=0):
    return pl.CostEstimate(flops=flops, bytes_accessed=nbytes, transcendentals=exps)


def shaped(shape, dtype=bf16):
    return jax.ShapeDtypeStruct(shape, dtype)


def forward(cut, pos, x, pieces):
    return pl.pallas_call(
        forward_kernel,
        grid=(SLOTS // STEP,),
        in_specs=[smem, smem, rows_spec(D)] + [whole(2, 2, 4, BLK, BLK)] * 8,
        out_specs=[rows_spec(3 * COLS), rows_spec(COLS), p_spec, whole(D, 3 * COLS), whole(D, COLS)],
        out_shape=[
            shaped((TOK, 3 * COLS)),
            shaped((TOK, COLS)),
            shaped((SLOTS, HEADS_DEV, WIN, WIN), f32),
            shaped((D, 3 * COLS)),
            shaped((D, COLS)),
        ],
        compiler_params=params(),
        cost_estimate=cost(2 * TOK * D * 4 * COLS, 25 << 20, SLOTS * HEADS_DEV * WIN * WIN),
        name="attention_forward",
    )(cut, pos, x, *pieces)


def backward(cot, qkv, p, wo):
    return pl.pallas_call(
        backward_kernel,
        grid=(SLOTS // STEP,),
        in_specs=[rows_spec(D), rows_spec(3 * COLS), p_spec, whole(D, COLS)],
        out_specs=rows_spec(3 * COLS),
        out_shape=shaped((TOK, 3 * COLS)),
        compiler_params=params(),
        cost_estimate=cost(2 * TOK * D * 4 * COLS, 25 << 20),
        name="attention_backward",
    )(cot, qkv, p, wo)


def grads(chips, core, x, cot, dp, att):
    count = len(chips)
    return pl.pallas_call(
        grads_kernel,
        grid_spec=pltpu.PrefetchScalarGridSpec(
            num_scalar_prefetch=1,
            grid=(count,),
            in_specs=[
                pl.BlockSpec((TOK, 2 * BLK), lambda i, where: (0, where[i])),
                pl.BlockSpec((TOK, 2 * BLK), lambda i, where: (0, where[i])),
                whole(TOK, 3 * COLS),
                whole(TOK, COLS),
            ],
            out_specs=[whole(2, 2, 4, BLK, BLK)] * count,
        ),
        out_shape=[shaped((2, 2, 4, BLK, BLK))] * count,
        compiler_params=params(),
        cost_estimate=cost(count * TOK * D * COLS, 8 << 20),
        name="weight_gradients",
    )(jnp.stack(list(chips) + [core]), x, cot, dp, att)


def project(a, w):
    depth = a.shape[1]
    return pl.pallas_call(
        project_kernel,
        grid=(SLOTS // STEP,),
        in_specs=[rows_spec(depth), whole(D, depth)],
        out_specs=[own_spec, sib_spec],
        out_shape=[shaped((TOK // 2, D)), shaped((TOK // 2, D))],
        compiler_params=params(),
        cost_estimate=cost(2 * TOK * D * depth, 8 << 20),
        name="project",
    )(a, w)


def finish(where, parts):
    return pl.pallas_call(
        finish_kernel,
        grid_spec=pltpu.PrefetchScalarGridSpec(
            num_scalar_prefetch=1,
            grid=(4,),
            in_specs=[pl.BlockSpec((1, 4, BLK, BLK), lambda s, where: (s, 0, 0, 0))] * 4,
            out_specs=[
                pl.BlockSpec((3, 4 * BLK, BLK), lambda s, where: (0, where[s], 0)),
                pl.BlockSpec((BLK, 4 * BLK), lambda s, where: (0, where[s])),
            ],
        ),
        out_shape=[shaped((3, D, BLK), f32), shaped((BLK, D), f32)],
        compiler_params=params(),
        cost_estimate=cost(0, 8 << 20),
        name="finish_gradients",
    )(where, *parts)


def shift(x, axes, by):
    count = lax.axis_size(axes)
    return lax.ppermute(x, axes, [(i, (i + by) % count) for i in range(count)])


def swap(x, axes, mask):
    count = lax.axis_size(axes)
    return lax.ppermute(x, axes, [(i, i ^ mask) for i in range(count)])


def shift_both(x, by):
    rows, cols = lax.axis_size(ROW), lax.axis_size(LON)
    pairs = [
        (r * cols + c, (r + by) % rows * cols + (c + by) % cols)
        for r in range(rows)
        for c in range(cols)
    ]
    return lax.ppermute(x, ALL, pairs)


def after(x, *deps):
    return lax.optimization_barrier((x,) + deps)[0]


def roll_in_start(x):
    x = x.transpose(0, 2, 1, 3)
    lon = WLON // 2
    corner = shift_both(x[:CLAT, :lon], -1)
    below = shift(x[:CLAT, lon:], ROW, -1)
    right = shift(x[CLAT:, :lon], LON, -1)
    return x[CLAT:, lon:], right, below, corner


def roll_in_end(own, right, below, corner):
    top = jnp.concatenate([own, right], axis=1)
    bottom = jnp.concatenate([below, corner], axis=1)
    return jnp.concatenate([top, bottom], axis=0).reshape(WIN, D)


def roll_out(x):
    x = x.reshape(2 * CLAT, WLON, LEV, D)
    lon = WLON // 2
    corner = shift_both(x[CLAT:, lon:], 1)
    above = shift(x[CLAT:, :lon], ROW, 1)
    left = shift(x[:CLAT, lon:], LON, 1)
    top = jnp.concatenate([corner, above], axis=1)
    bottom = jnp.concatenate([left, x[:CLAT, :lon]], axis=1)
    return jnp.concatenate([top, bottom], axis=0).transpose(0, 2, 1, 3)


def normalize(tokens):
    values = tokens.astype(f32)
    average = jnp.mean(values, -1, keepdims=True)
    centered = values - average
    inverse_std = lax.rsqrt(jnp.mean(centered * centered, -1, keepdims=True) + EPSILON)
    return centered * inverse_std, inverse_std


def share_start(x, first, second):
    return x, swap(x, NEAR, first), swap(x, NEAR, second), swap(x, "core", 1)


def share_end(started, first, second):
    x, one, two, sibling = started
    parts = {0: x, first: one, second: two, 3: swap(one, NEAR, second)}
    mine = [parts[s] for s in range(4)]
    theirs = [sibling] + [swap(part, "core", 1) for part in mine[1:]]
    return jnp.concatenate(mine + theirs, axis=0)


def collect_start(own, sib, first, second):
    own = own.reshape(4, WIN, D)
    sib = sib.reshape(4, WIN, D)
    sums = {}
    for s in (3, first, second, 0):
        sums[s] = own[s].astype(f32) + swap(sib[s], "core", 1).astype(f32)
    sums = {s: total.astype(bf16) for s, total in sums.items()}
    return {
        "sums": sums,
        "far": swap(sums[3], NEAR, first),
        "first": swap(sums[first], NEAR, first),
        "mid": sums[second],
        "own": sums[0],
    }


def collect_mid(parts, dep, second):
    far = after(parts["far"], dep)
    send = (parts["mid"].astype(f32) + far.astype(f32)).astype(bf16)
    return dict(parts, send=send, second=swap(send, NEAR, second))


def collect_end(parts, dep):
    one, two = after((parts["first"], parts["second"]), dep)
    return (parts["own"].astype(f32) + one.astype(f32) + two.astype(f32)).astype(bf16)


def weight_units(w_qkv, w_out, place):
    qkv = lax.dynamic_slice(w_qkv.transpose(1, 0, 2), (0, place * BLK, 0), (3, BLK, BLK))
    out = lax.dynamic_slice(w_out, (0, place * BLK), (BLK, BLK)).T
    unit = jnp.concatenate([qkv, out[None]], axis=0)
    return [unit] + [swap(unit, "zh", s) for s in (1, 2, 3)]


def spread_weights(mine, near):
    pieces = {(0, 0): mine, (0, 1): near}
    for t, part in ((0, mine), (1, near)):
        for s in (1, 3):
            pieces[s, t] = swap(part, "lat", s)
    pieces[2, 0] = swap(pieces[1, 0], "lat", 3)
    pieces[2, 1] = swap(pieces[3, 1], "lat", 1)
    return pieces


def sum_everywhere(x):
    for axes in (LON, "lat", "zh", NEAR):
        one, two, three = (swap(x, axes, s) for s in (1, 2, 3))
        x = (x + one) + (two + three)
    return x


def shards(tokens, norm_gain, w_qkv, w_out, grad_out):
    zh, lat, xl, core = (lax.axis_index(a) for a in ("zh", "lat", "xl", "core"))
    half = (zh // 2) ^ core
    chips = {(s, t): (lat ^ s) * 2 + (xl ^ t) for s in range(4) for t in range(2)}
    places = sorted(chips)
    pos = jnp.stack([chips[place] * 2 + (core ^ c) for place in places for c in range(2)])
    ends = jnp.stack(
        [lat ^ s for s in range(4)] + [(xl ^ t) * 2 + (core ^ c) for c in range(2) for t in range(2)]
    )
    edge = jnp.logical_and(zh == 3, lat == 3)
    owners = lax.axis_index(NEAR) ^ (jnp.arange(SLOTS) % 4)
    cut = jnp.logical_and(edge, owners == 3).astype(jnp.int32)

    units = weight_units(w_qkv, w_out, pos[0])
    rolling = roll_in_start(tokens)
    low, high = jnp.stack(units[:2]), jnp.stack(units[2:])
    keep = jnp.where(half == 0, low, high)
    give = jnp.where(half == 0, high, low)
    given = swap(give, "core", 1)
    rolled = roll_in_end(*after(rolling, give))
    standard, inverse_std = normalize(rolled)
    normed = (standard * norm_gain).astype(bf16)
    sharing = share_start(normed, 1, 2)
    mine = jnp.stack([keep, after(given, normed)])
    near = swap(mine, "xl", 1)
    turning = roll_in_start(after(grad_out, mine))
    near = after(near, turning)
    pieces = spread_weights(mine, near)
    x = share_end(after(sharing, near), 1, 2)
    cotangent = roll_in_end(*after(turning, sharing[1]))
    cot = share_end(share_start(cotangent, 2, 1), 2, 1)

    qkv, att, p, wq, wo = forward(cut, pos, x, [pieces[place] for place in places])
    dp = backward(cot, qkv, p, wo)
    far = grads([chips[2, 0], chips[2, 1]], core, x, cot, dp, att)
    back = {3: swap(far[0], "lat", 1), 1: swap(far[1], "lat", 3)}
    g10, g11, g30, g31 = grads(
        [chips[1, 0], chips[1, 1], chips[3, 0], chips[3, 1]], core, x, cot, dp, att
    )
    g00, g01 = grads([chips[0, 0], chips[0, 1]], core, after(x, g10), cot, dp, att)
    back = after(back, g00)
    g11 = (g11.astype(f32) + back[1].astype(f32)).astype(bf16)
    g30 = (g30.astype(f32) + back[3].astype(f32)).astype(bf16)
    sent1 = swap(g10, "lat", 1), swap(g11, "lat", 1)
    sent3 = swap(g30, "lat", 3), swap(g31, "lat", 3)

    d_own, d_sib = project(after(dp, g11, g30), wq)
    b_own, b_sib = project(after(att, d_own), wo)
    d_parts = collect_start(d_own, after(d_sib, b_own), 2, 1)
    sent1, sent3, _ = lax.optimization_barrier((sent1, sent3, d_parts["sums"]))
    t1 = (g01.astype(f32) + sent1[1].astype(f32) + sent3[1].astype(f32)).astype(bf16)
    t0 = g00.astype(f32) + sent1[0].astype(f32) + sent3[0].astype(f32)
    crossing = swap(t1, "xl", 1)
    b_parts = collect_start(b_own, after(b_sib, t1), 1, 2)
    t0 = t0 + after(crossing, b_parts["sums"]).astype(f32)
    ours = t0[0].astype(bf16)
    to_core = t0[1].astype(bf16)
    theirs = swap(to_core, "core", 1)
    d_parts = collect_mid(d_parts, to_core, 1)
    theirs = after(theirs, d_parts["send"])
    low = jnp.where(half == 0, ours, theirs)
    high = jnp.where(half == 0, theirs, ours)
    back = [swap(low[1], "zh", 1), swap(high[0], "zh", 2), swap(high[1], "zh", 3)]
    b_parts = collect_mid(b_parts, low, 2)
    back = after(back, b_parts["send"])
    unit = low[0].astype(f32) + back[0].astype(f32) + back[1].astype(f32) + back[2].astype(f32)
    unit = unit.astype(bf16)
    rows = [swap(unit, "lat", s) for s in (1, 2, 3)]

    d_normed = collect_end(d_parts, unit)
    d_normed = d_normed.astype(f32)
    gain_local = jnp.sum(d_normed * standard, 0).reshape(16, BLK)
    scaled = d_normed * norm_gain
    d_local = inverse_std * (
        scaled
        - jnp.mean(scaled, -1, keepdims=True)
        - standard * jnp.mean(scaled * standard, -1, keepdims=True)
    )
    grad_tokens = (cotangent.astype(f32) + d_local).astype(bf16)
    rows = jnp.stack([unit] + after(rows, grad_tokens))
    near_rows = swap(rows, "xl", 1)
    core_rows = swap(rows, "core", 1)
    branch = collect_end(b_parts, rows)
    output = (rolled.astype(f32) + branch.astype(f32)).astype(bf16)
    near_rows = after(near_rows, output)
    last_rows = swap(near_rows, "core", 1)
    gain_sum = sum_everywhere(gain_local)
    grad_tokens = roll_out(grad_tokens)
    output = roll_out(output)
    grad_wqkv, grad_wout = finish(ends, [rows, near_rows, core_rows, last_rows])
    return output, grad_tokens, grad_wqkv.transpose(1, 0, 2), grad_wout, gain_sum.reshape(D)


def solution(mesh):
    fine = Mesh(mesh.devices.reshape(4, 2, 2, 4, 2, 2), ALL)
    by_token = P(ROW, None, LON, None)
    in_specs = (by_token, P(), P(None, None, OUTER), P(OUTER, None), by_token)
    out_specs = (by_token, by_token, P(None, None, OUTER), P(OUTER, None), P())
    return jax.shard_map(shards, mesh=fine, in_specs=in_specs, out_specs=out_specs, check_vma=False)
```

```python
import functools

import jax
import jax.numpy as jnp
from jax import lax
from jax.experimental import pallas as pl
from jax.experimental.pallas import tpu as pltpu
from jax.sharding import Mesh, PartitionSpec as P

D = 2048
HEAD = 64
LEV = 2
CLAT = 3
WLON = 12
WIN = 2 * CLAT * LEV * WLON
HALF = WIN // 2
SLOTS = 8
STEP = 2
ROWS = STEP * WIN
TOK = SLOTS * WIN
COLS = 256
HEADS_DEV = COLS // HEAD
SCALE = HEAD ** (-0.5)
BLK = 128
EPSILON = 1e-05
bf16 = jnp.bfloat16
f32 = jnp.float32

ALL = ("zh", "zl", "xh", "lat", "xl", "core")
OUTER = ("zh", "zl", "xh")
ROW = ("zh", "zl", "xh", "lat")
LON = ("xl", "core")
NEAR = ("zl", "xh")


def nn(a, b):
    return lax.dot_general(a, b, (((1,), (0,)), ((), ())), preferred_element_type=f32)


def nt(a, b):
    return lax.dot_general(a, b, (((1,), (1,)), ((), ())), preferred_element_type=f32)


def tn(a, b):
    return lax.dot_general(a, b, (((0,), (0,)), ((), ())), preferred_element_type=f32)


def assemble(pos_ref, pieces, wq_ref, wo_ref):
    for n, piece in enumerate(pieces):
        for c in range(2):
            rows = pl.ds(pl.multiple_of(pos_ref[2 * n + c] * BLK, BLK), BLK)
            for blk in range(2):
                for i in range(3):
                    wq_ref[rows, (2 * i + blk) * BLK : (2 * i + blk + 1) * BLK] = piece[c, blk, i]
                wo_ref[rows, blk * BLK : (blk + 1) * BLK] = piece[c, blk, 3]


def choose(step, own_ref, sib_ref, out_ref):
    @pl.when(step < HALF_STEPS)
    def _():
        out_ref[...] = own_ref[...]

    @pl.when(step >= HALF_STEPS)
    def _():
        out_ref[...] = sib_ref[...]


def forward_kernel(cut_ref, pos_ref, own_ref, sib_ref, *refs):
    pieces, (qkv_ref, att_ref, p_ref, wq_ref, wo_ref, x_ref) = refs[:8], refs[8:]
    step = pl.program_id(0)

    @pl.when(step == 0)
    def _():
        assemble(pos_ref, pieces, wq_ref, wo_ref)

    choose(step, own_ref, sib_ref, x_ref)
    for n in range(3):
        cols = slice(n * COLS, (n + 1) * COLS)
        qkv_ref[:, cols] = nn(x_ref[...], wq_ref[:, cols]).astype(bf16)
    row = lax.broadcasted_iota(jnp.int32, (WIN, WIN), 0) >= HALF
    col = lax.broadcasted_iota(jnp.int32, (WIN, WIN), 1) >= HALF
    same = row == col
    for w in range(STEP):
        rows = slice(w * WIN, (w + 1) * WIN)
        allowed = jnp.logical_or(same, cut_ref[step * STEP + w] == 0)
        for h in range(HEADS_DEV):
            q = qkv_ref[rows, h * HEAD : (h + 1) * HEAD]
            k = qkv_ref[rows, COLS + h * HEAD : COLS + (h + 1) * HEAD]
            v = qkv_ref[rows, 2 * COLS + h * HEAD : 2 * COLS + (h + 1) * HEAD]
            s = jnp.where(allowed, nt(q, k) * SCALE, -1e30)
            e = jnp.exp(s - jnp.max(s, -1, keepdims=True))
            p = e / jnp.sum(e, -1, keepdims=True)
            p_ref[w, h] = p
            att_ref[rows, h * HEAD : (h + 1) * HEAD] = nn(p.astype(bf16), v).astype(bf16)


def backward_kernel(own_ref, sib_ref, qkv_ref, p_ref, wo_ref, _, dp_ref, sent_ref, cot_ref):
    choose(pl.program_id(0), own_ref, sib_ref, cot_ref)
    d_att = nn(cot_ref[...], wo_ref[...]).astype(bf16)
    for w in range(STEP):
        rows = slice(w * WIN, (w + 1) * WIN)
        for h in range(HEADS_DEV):
            q = qkv_ref[rows, h * HEAD : (h + 1) * HEAD]
            k = qkv_ref[rows, COLS + h * HEAD : COLS + (h + 1) * HEAD]
            v = qkv_ref[rows, 2 * COLS + h * HEAD : 2 * COLS + (h + 1) * HEAD]
            p = p_ref[w, h]
            d_o = d_att[rows, h * HEAD : (h + 1) * HEAD]
            d_w = nt(d_o, v)
            dots = jnp.sum(p * d_w, -1, keepdims=True)
            d_s = (p * (d_w - dots) * SCALE).astype(bf16)
            dp_ref[rows, h * HEAD : (h + 1) * HEAD] = nn(d_s, k).astype(bf16)
            dp_ref[rows, COLS + h * HEAD : COLS + (h + 1) * HEAD] = tn(d_s, q).astype(bf16)
            dp_ref[rows, 2 * COLS + h * HEAD : 2 * COLS + (h + 1) * HEAD] = tn(p.astype(bf16), d_o).astype(bf16)

    @pl.when(pl.program_id(0) >= HALF_STEPS)
    def _():
        sent_ref[...] = dp_ref[...]


def grads_kernel(count, where_ref, xa_ref, xb_ref, ca_ref, cb_ref, dp_ref, att_ref, _, *refs):
    step = pl.program_id(0)
    core = where_ref[count]
    g_refs, (x_ref, cot_ref) = refs[:count], refs[count:]
    x_ref[:PART, :], x_ref[PART:, :] = xa_ref[...], xb_ref[...]
    cot_ref[:PART, :], cot_ref[PART:, :] = ca_ref[...], cb_ref[...]
    gq = tn(x_ref[...], dp_ref[...]).astype(bf16)
    go = tn(cot_ref[...], att_ref[...]).astype(bf16)
    for n, g_ref in enumerate(g_refs):

        @pl.when(step == n)
        def _():
            for part in range(2):
                rows = slice(part * BLK, (part + 1) * BLK)
                place = part ^ core
                for blk in range(2):
                    for i in range(3):
                        g_ref[place, blk, i] = gq[rows, (2 * i + blk) * BLK : (2 * i + blk + 1) * BLK]
                    g_ref[place, blk, 3] = go[rows, blk * BLK : (blk + 1) * BLK]


def product(lead, out, pair, slots):
    for n, (ref, at) in enumerate(slots):
        target = pair if ref else lead
        target[at * WIN : (at + 1) * WIN, :] = out[n * WIN : (n + 1) * WIN, :]


def rolled_kernel(dp_ref, in_ref, w_ref, other_ref, x_ref, _, lead_ref, pair_ref, gain_ref):
    total = nt(dp_ref[...], w_ref[...]) + nt(in_ref[...], other_ref[...])
    product(lead_ref, total.astype(bf16), pair_ref, ((0, 0), (0, 1), (1, 0), (1, 1)))
    gain_ref[...] = jnp.sum(total * x_ref[...].astype(f32), 0, keepdims=True)


def branch_kernel(att_ref, w_ref, _, own_ref, sib_ref):
    total = nt(att_ref[...], w_ref[...]).astype(bf16)
    own_ref[...] = total[:PART]
    sib_ref[...] = total[PART:]


def finish_kernel(where_ref, a_ref, b_ref, c_ref, d_ref, gain, gain_in, gq_ref, go_ref, gain_out):
    gain_out[...] = gain[...] + gain_in[...]
    for n, ref in enumerate((a_ref, b_ref, c_ref, d_ref)):
        rows = pl.ds(pl.multiple_of(where_ref[4 + n] * BLK, BLK), BLK)
        for i in range(3):
            gq_ref[i, rows, :] = ref[0, i].astype(f32)
        go_ref[:, rows] = ref[0, 3].astype(f32).T


def params():
    return pltpu.CompilerParams(dimension_semantics=("arbitrary",), vmem_limit_bytes=63 * 1024 * 1024)


PART = TOK // 2
HALF_STEPS = SLOTS // STEP // 2
own_spec = pl.BlockSpec((ROWS, D), lambda i: (jnp.minimum(i, HALF_STEPS - 1), 0))
sib_spec = pl.BlockSpec((ROWS, D), lambda i: (jnp.maximum(i - HALF_STEPS, 0), 0))
p_spec = pl.BlockSpec((STEP, HEADS_DEV, WIN, WIN), lambda i: (i, 0, 0, 0))
smem = pl.BlockSpec(memory_space=pltpu.SMEM)
unread = pl.BlockSpec(memory_space=pl.ANY)
column = pl.BlockSpec((PART, 2 * BLK), lambda i: (0, i))


def rows_spec(cols):
    return pl.BlockSpec((ROWS, cols), lambda i: (i, 0))


def later_spec(cols):
    return pl.BlockSpec((ROWS, cols), lambda i: (jnp.maximum(i - HALF_STEPS, 0), 0))


def whole(*shape):
    return pl.BlockSpec(shape, lambda *i: (0,) * len(shape))


def shaped(shape, dtype=bf16):
    return jax.ShapeDtypeStruct(shape, dtype)


def forward(cut, pos, own, sib, weights):
    return pl.pallas_call(
        forward_kernel,
        grid=(SLOTS // STEP,),
        in_specs=[smem, smem, own_spec, sib_spec] + [whole(*w.shape) for w in weights],
        out_specs=[
            rows_spec(3 * COLS),
            rows_spec(COLS),
            p_spec,
            whole(D, 3 * COLS),
            whole(D, COLS),
        ],
        out_shape=[
            shaped((TOK, 3 * COLS)),
            shaped((TOK, COLS)),
            shaped((SLOTS, HEADS_DEV, WIN, WIN), f32),
            shaped((D, 3 * COLS)),
            shaped((D, COLS)),
        ],
        scratch_shapes=[pltpu.VMEM((ROWS, D), bf16)],
        compiler_params=params(),
        name="attention_forward",
    )(cut, pos, own, sib, *weights)


def backward(own, sib, qkv, p, wo, before):
    return pl.pallas_call(
        backward_kernel,
        grid=(SLOTS // STEP,),
        in_specs=[own_spec, sib_spec, rows_spec(3 * COLS), p_spec, whole(D, COLS), unread],
        out_specs=[rows_spec(3 * COLS), later_spec(3 * COLS)],
        out_shape=[shaped((TOK, 3 * COLS)), shaped((PART, 3 * COLS))],
        scratch_shapes=[pltpu.VMEM((ROWS, D), bf16)],
        compiler_params=params(),
        name="attention_backward",
    )(own, sib, qkv, p, wo, before)


def grads(chips, core, xs, cots, dp, att, before):
    count = len(chips)
    part = pl.BlockSpec((PART, 2 * BLK), lambda i, where: (0, where[i]))
    return pl.pallas_call(
        functools.partial(grads_kernel, count),
        grid_spec=pltpu.PrefetchScalarGridSpec(
            num_scalar_prefetch=1,
            grid=(count,),
            in_specs=[part] * 4 + [whole(TOK, 3 * COLS), whole(TOK, COLS), unread],
            out_specs=[whole(2, 2, 4, BLK, BLK)] * count,
            scratch_shapes=[pltpu.VMEM((TOK, 2 * BLK), bf16)] * 2,
        ),
        out_shape=[shaped((2, 2, 4, BLK, BLK))] * count,
        compiler_params=params(),
        name="weight_gradients",
    )(jnp.stack(list(chips) + [core]), *xs, *cots, dp, att, before)


def rolled_gradient(dp, dp_in, wq, wq_in, x, before):
    depth = 3 * COLS
    strip = pl.BlockSpec((2 * BLK, depth), lambda i: (i, 0))
    half = pl.BlockSpec((PART // 2, 2 * BLK), lambda i: (0, i))
    return pl.pallas_call(
        rolled_kernel,
        grid=(8,),
        in_specs=[whole(PART, depth)] * 2 + [strip] * 2 + [column, unread],
        out_specs=[half, half, pl.BlockSpec((1, 2 * BLK), lambda i: (0, i))],
        out_shape=[shaped((PART // 2, D))] * 2 + [shaped((1, D), f32)],
        compiler_params=params(),
        name="rolled_gradient",
    )(dp, dp_in, wq, wq_in, x, before)


def branch_product(att, wo, before):
    return pl.pallas_call(
        branch_kernel,
        grid=(8,),
        in_specs=[whole(TOK, COLS), pl.BlockSpec((2 * BLK, COLS), lambda i: (i, 0)), unread],
        out_specs=[column, column],
        out_shape=[shaped((PART, D))] * 2,
        compiler_params=params(),
        name="branch_product",
    )(att, wo, before)


def finish(where, parts, gain, gain_in):
    return pl.pallas_call(
        finish_kernel,
        grid_spec=pltpu.PrefetchScalarGridSpec(
            num_scalar_prefetch=1,
            grid=(4,),
            in_specs=[pl.BlockSpec((1, 4, BLK, BLK), lambda s, where: (s, 0, 0, 0))] * 4 + [whole(16, BLK)] * 2,
            out_specs=[
                pl.BlockSpec((3, 4 * BLK, BLK), lambda s, where: (0, where[s], 0)),
                pl.BlockSpec((BLK, 4 * BLK), lambda s, where: (0, where[s])),
                whole(16, BLK),
            ],
        ),
        out_shape=[shaped((3, D, BLK), f32), shaped((BLK, D), f32), shaped((16, BLK), f32)],
        compiler_params=params(),
        name="finish_gradients",
    )(where, *parts, gain, gain_in)


def small(body, ins, outs, before=(), specs=(), scratch=(), name=None):
    specs = dict(specs)
    in_specs = [specs.get(n, whole(*x.shape)) for n, x in enumerate(ins)] + [unread] * len(before)
    count, extra = len(ins), len(before)

    def kernel(*refs):
        body(*refs[:count], *refs[count + extra :])

    return pl.pallas_call(
        kernel,
        grid=(1,),
        in_specs=in_specs,
        out_specs=[whole(*x.shape) for x in outs],
        out_shape=list(outs),
        scratch_shapes=list(scratch),
        compiler_params=params(),
        name=name,
    )(*ins, *before)


QUARTER = WIN // 4
UNIT = (4, BLK, BLK)
PAIR = (2,) + UNIT
FOUR = (2, 2) + UNIT
GAIN = (16, BLK)


def wide(*refs):
    total = refs[0].astype(f32)
    for ref in refs[1:]:
        total = total + ref.astype(f32)
    return total


def add_low(*values):
    return wide(*values).astype(bf16)


def select_body(half_ref, u0, u1, u2, u3, keep, give):
    @pl.when(half_ref[0] == 0)
    def _():
        keep[0], keep[1], give[0], give[1] = u0[...], u1[...], u2[...], u3[...]

    @pl.when(half_ref[0] != 0)
    def _():
        keep[0], keep[1], give[0], give[1] = u2[...], u3[...], u0[...], u1[...]


def join_body(*refs):
    out = refs[-1]
    for n, ref in enumerate(refs[:-1]):
        out[n] = ref[...]


def rows_body(*refs):
    out = refs[-1]
    for n, ref in enumerate(refs[:-1]):
        out[n * WIN : (n + 1) * WIN, :] = ref[...]


def pin_body(out):
    out[...] = jnp.zeros_like(out)


def normal(values):
    centered = values - jnp.mean(values, -1, keepdims=True)
    inverse_std = lax.rsqrt(jnp.mean(centered * centered, -1, keepdims=True) + EPSILON)
    return centered * inverse_std, inverse_std


def enter_body(own, right, below, corner, gain, rolled, cot, normed, buffer):
    for n, out in enumerate((rolled, cot)):
        for k, piece in enumerate((own, right, below, corner)):
            buffer[k * QUARTER : (k + 1) * QUARTER, :] = piece[n].astype(f32)
        out[...] = buffer[...].astype(bf16)
        if n == 0:
            normed[...] = (normal(buffer[...])[0] * gain[...]).astype(bf16)


def leave_body(rolled, cot, gain, b0, b1, b2, d0, d1, d2, sums, sums_in, own, right, below, corner, sums_out, buffer):
    sums_out[...] = sums[...] + sums_in[...]
    branch = add_low(b0[...], b1[...], b2[...])
    buffer[...] = rolled[...].astype(f32) + branch.astype(f32)
    for k, piece in enumerate((own, right, below, corner)):
        piece[0] = buffer[k * QUARTER : (k + 1) * QUARTER, :].astype(bf16)
    standard, inverse_std = normal(rolled[...].astype(f32))
    scaled = add_low(d0[...], d1[...], d2[...]).astype(f32) * gain[...]
    local = inverse_std * (
        scaled
        - jnp.mean(scaled, -1, keepdims=True)
        - standard * jnp.mean(scaled * standard, -1, keepdims=True)
    )
    buffer[...] = cot[...].astype(f32) + local
    for k, piece in enumerate((own, right, below, corner)):
        piece[1] = buffer[k * QUARTER : (k + 1) * QUARTER, :].astype(bf16)


def windows_body(own, other, lead, pair):
    for n, (out, at) in enumerate(((lead, 0), (pair, 0), (lead, 1), (pair, 1))):
        rows = slice(n * WIN, (n + 1) * WIN)
        out[at * WIN : (at + 1) * WIN, :] = add_low(own[rows, :], other[rows, :])


def mid_body(lead, given, out):
    out[...] = add_low(lead[...], given[...])


def gain_mid_body(lead, given, gain, gain_in, out, gain_out):
    mid_body(lead, given, out)
    gain_out[...] = gain[...] + gain_in[...]


def sides_body(g10, g11, g30, g31, back1, back3, to1, to3):
    to1[0], to1[1] = g10[...], add_low(g11[...], back1[...])
    to3[0], to3[1] = add_low(g30[...], back3[...]), g31[...]


def lat_body(g00, g01, in1, in3, gain, gain_in, t0, t1, gain_out):
    t0[...] = add_low(g00[...], in1[0], in3[0])
    t1[...] = add_low(g01[...], in1[1], in3[1])
    gain_out[...] = gain[...] + gain_in[...]


def xl_body(t0, crossing, gain, gain_in, ours, others, gain_out):
    ours[...] = add_low(t0[0], crossing[0])
    others[...] = add_low(t0[1], crossing[1])
    gain_out[...] = gain[...] + gain_in[...]


def core_body(half_ref, ours, theirs, gain, gain_in, s0, s1, s2, s3, gain_out):
    gain_out[...] = gain[...] + gain_in[...]

    @pl.when(half_ref[0] == 0)
    def _():
        s0[...], s1[...], s2[...], s3[...] = ours[0], ours[1], theirs[0], theirs[1]

    @pl.when(half_ref[0] != 0)
    def _():
        s0[...], s1[...], s2[...], s3[...] = theirs[0], theirs[1], ours[0], ours[1]


def zh_body(kept, b1, b2, b3, unit):
    unit[...] = add_low(kept[...], b1[...], b2[...], b3[...])


def rows_gain_body(u0, u1, u2, u3, gain, gain_in, rows, gain_out):
    rows[0], rows[1], rows[2], rows[3] = u0[...], u1[...], u2[...], u3[...]
    gain_out[...] = gain[...] + gain_in[...]


def shift(x, axes, by):
    count = lax.axis_size(axes)
    return lax.ppermute(x, axes, [(i, (i + by) % count) for i in range(count)])


def swap(x, axes, mask):
    count = lax.axis_size(axes)
    return lax.ppermute(x, axes, [(i, i ^ mask) for i in range(count)])


def shift_both(x, by):
    rows, cols = lax.axis_size(ROW), lax.axis_size(LON)
    pairs = [
        (r * cols + c, (r + by) % rows * cols + (c + by) % cols)
        for r in range(rows)
        for c in range(cols)
    ]
    return lax.ppermute(x, ALL, pairs)


def quarters(*arrays):
    arrays = [x.transpose(0, 2, 1, 3) for x in arrays]
    lon = WLON // 2

    def cut(rows, cols):
        return jnp.stack([x[rows, cols].reshape(QUARTER, D) for x in arrays])

    first, last = slice(0, CLAT), slice(CLAT, 2 * CLAT)
    west, east = slice(0, lon), slice(lon, WLON)
    below = shift(cut(first, east), ROW, -1)
    corner = shift_both(cut(first, west), -1)
    right = shift(cut(last, west), LON, -1)
    return cut(last, east), right, below, corner


def back_home(before, own, right, below, corner):
    below, corner, right = shift(below, ROW, 1), shift_both(corner, 1), shift(right, LON, 1)
    below, corner, right, _ = lax.optimization_barrier((below, corner, right, before))
    own, right, below, corner = (
        x.reshape(2, CLAT, WLON // 2, LEV, D) for x in (own, right, below, corner)
    )
    top = jnp.concatenate([corner, below], axis=2)
    bottom = jnp.concatenate([right, own], axis=2)
    both = jnp.concatenate([top, bottom], axis=1).transpose(0, 1, 3, 2, 4)
    return both[0], both[1]


def weight_unit(w_qkv, w_out, place):
    qkv = lax.dynamic_slice(w_qkv.transpose(1, 0, 2), (0, place * BLK, 0), (3, BLK, BLK))
    out = lax.dynamic_slice(w_out, (0, place * BLK), (BLK, BLK)).T
    return jnp.concatenate([qkv, out[None]], axis=0)


def shards(tokens, norm_gain, w_qkv, w_out, grad_out):
    zh, lat, xl, core = (lax.axis_index(a) for a in ("zh", "lat", "xl", "core"))
    half = ((zh // 2) ^ core).reshape(1)
    chips = {(s, t): (lat ^ s) * 2 + (xl ^ t) for s in range(4) for t in range(2)}
    pos = jnp.stack([chips[place] * 2 + (core ^ c) for place in sorted(chips) for c in range(2)])
    ends = jnp.stack(
        [lat ^ s for s in range(4)] + [(xl ^ t) * 2 + (core ^ c) for c in range(2) for t in range(2)]
    )
    edge = jnp.logical_and(zh == 3, lat == 3)
    owners = lax.axis_index(NEAR) ^ (jnp.arange(SLOTS) % 4)
    cut = jnp.logical_and(edge, owners == 3).astype(jnp.int32)
    gain_row = norm_gain.reshape(1, D)
    token = shaped((8, BLK), f32)
    window, windows = shaped((WIN, D)), shaped((4 * WIN, D))
    scalar = {0: smem}

    unit = weight_unit(w_qkv, w_out, pos[0])
    units = [unit] + [swap(unit, "zh", s) for s in (1, 2, 3)]
    pieces = quarters(tokens, grad_out)
    keep, give = small(select_body, [half] + units, [shaped(PAIR)] * 2, specs=scalar, name="select")
    given = swap(give, "core", 1)
    buffer = [pltpu.VMEM((WIN, D), f32)]
    rolled, cotangent, normed = small(
        enter_body, [*pieces, gain_row], [window] * 3, before=[give], scratch=buffer, name="enter"
    )
    (mine,) = small(join_body, [keep, given], [shaped(FOUR)], before=[normed], name="join")
    near = swap(mine, "xl", 1)
    m1a, m3a = swap(mine, "lat", 1), swap(mine, "lat", 3)
    x1, x2 = swap(normed, NEAR, 1), swap(normed, NEAR, 2)
    (pin,) = small(pin_body, [], [token], before=[near, m1a, m3a], name="pin")
    m1b, m3b = swap(near, "lat", 1), swap(near, "lat", 3)
    o0 = swap(m1a, "lat", 3)
    (pin,) = small(pin_body, [], [token], before=[m1b, m3b, x1, x2, pin], name="pin")
    o1 = swap(m3b, "lat", 1)
    x3 = swap(lax.optimization_barrier((x1, pin))[0], NEAR, 2)
    (x_own,) = small(rows_body, [normed, x1, x2, x3], [windows], before=[o0, o1, pin], name="rows")
    x_sib = swap(x_own, "core", 1)
    c1, c2, c3 = (swap(cotangent, NEAR, s) for s in (1, 2, 3))

    weights = [mine, near, m1a, m1b, o0, o1, m3a, m3b]
    qkv, att, p, wq, wo = forward(cut, pos, x_own, x_sib, weights)
    (c_own,) = small(rows_body, [cotangent, c1, c2, c3], [windows], before=[wo], name="rows")
    c_sib = swap(c_own, "core", 1)
    b_own, b_sib = branch_product(att, wo, c_own)
    b_other = swap(b_sib, "core", 1)
    wq_in = swap(lax.optimization_barrier((wq, b_own))[0], "core", 1)
    dp, dp_sent = backward(c_own, c_sib, qkv, p, wo, b_own)
    dp_in = swap(dp_sent, "core", 1)
    xs, cots = (x_own, x_sib), (c_own, c_sib)

    far0, far1 = grads([chips[2, 0], chips[2, 1]], core, xs, cots, dp, att, dp)
    back3, back1 = swap(far0, "lat", 1), swap(far1, "lat", 3)
    near_chips = [chips[s, t] for s in (1, 3, 0) for t in range(2)]
    g10, g11, g30, g31, g00, g01 = grads(near_chips, core, xs, cots, dp, att, far0)
    to1, to3 = small(
        sides_body, [g10, g11, g30, g31, back1, back3], [shaped((2,) + FOUR)] * 2, name="sides"
    )
    in1, in3 = swap(to1, "lat", 1), swap(to3, "lat", 3)
    first, second = pl.BlockSpec((WIN, D), lambda i: (0, 0)), pl.BlockSpec((WIN, D), lambda i: (1, 0))
    pair = shaped((2 * WIN, D))
    b_lead, b_pair = small(windows_body, [b_own, b_other], [pair] * 2, before=[to1], name="windows")
    b_in = swap(b_pair, NEAR, 1)
    d_lead, d_pair, gain = rolled_gradient(dp, dp_in, wq, wq_in, x_own, b_pair)
    d_in = swap(d_pair, NEAR, 2)

    gain, gain_shape = gain.reshape(GAIN), shaped(GAIN, f32)
    gain_in = swap(gain, ALL, 1)
    t0, t1, gain = small(
        lat_body,
        [g00, g01, in1, in3, gain, gain_in],
        [shaped(FOUR), shaped(FOUR), gain_shape],
        name="lat_sum",
    )
    crossing, gain_in = swap(t1, "xl", 1), swap(gain, ALL, 4)
    b_mid, gain = small(
        gain_mid_body,
        [b_lead, b_in, gain, gain_in],
        [window, gain_shape],
        before=[t1],
        specs={0: second, 1: second},
        name="mid",
    )
    b_last, gain_in = swap(b_mid, NEAR, 2), swap(gain, ALL, 2)
    ours, others, gain = small(
        xl_body,
        [t0, crossing, gain, gain_in],
        [shaped(PAIR)] * 2 + [gain_shape],
        before=[b_mid],
        name="xl_sum",
    )
    theirs, gain_in = swap(others, "core", 1), swap(gain, ALL, 8)
    (d_mid,) = small(
        mid_body, [d_lead, d_in], [window], before=[ours], specs={0: second, 1: second}, name="mid"
    )
    d_last = swap(d_mid, NEAR, 1)
    *sent, gain = small(
        core_body,
        [half, ours, theirs, gain, gain_in],
        [shaped(UNIT)] * 4 + [gain_shape],
        before=[d_mid],
        specs=scalar,
        name="core_sum",
    )
    back = [swap(sent[s], "zh", s) for s in (1, 2, 3)]
    (unit,) = small(zh_body, [sent[0], *back], [shaped(UNIT)], before=[b_last], name="zh_sum")
    around = [swap(unit, "lat", s) for s in (1, 2, 3)]
    gain_in = swap(lax.optimization_barrier((gain, unit))[0], ALL, 64)
    *results, gain = small(
        leave_body,
        [rolled, cotangent, gain_row, b_lead, b_in, b_last, d_lead, d_in, d_last, gain, gain_in],
        [shaped((2, QUARTER, D))] * 4 + [gain_shape],
        before=[unit],
        specs={n: first for n in (3, 4, 6, 7)},
        scratch=buffer,
        name="leave",
    )
    gain_in = swap(gain, ALL, 128)
    rows, gain = small(
        rows_gain_body,
        [unit, *around, gain, gain_in],
        [shaped((4,) + UNIT), gain_shape],
        name="slices",
    )
    near_rows, core_rows = swap(rows, "xl", 1), swap(rows, "core", 1)
    results, _ = lax.optimization_barrier((results, rows))
    output, grad_tokens = back_home(rows, *results)
    near_rows, output, _ = lax.optimization_barrier((near_rows, output, grad_tokens))
    last_rows = swap(near_rows, "core", 1)
    grad_wqkv, grad_wout, gain = finish(
        ends, [rows, near_rows, core_rows, last_rows], gain, swap(gain, ALL, 16)
    )
    grad_gain = (gain + swap(gain, ALL, 32)).reshape(D) / norm_gain
    return output, grad_tokens, grad_wqkv.transpose(1, 0, 2), grad_wout, grad_gain


def solution(mesh):
    fine = Mesh(mesh.devices.reshape(4, 2, 2, 4, 2, 2), ALL)
    by_token = P(ROW, None, LON, None)
    in_specs = (by_token, P(), P(None, None, OUTER), P(OUTER, None), by_token)
    out_specs = (by_token, by_token, P(None, None, OUTER), P(OUTER, None), P())
    return jax.shard_map(shards, mesh=fine, in_specs=in_specs, out_specs=out_specs, check_vma=False)
```

```python
import functools

import jax
import jax.numpy as jnp
from jax import lax
from jax.experimental import pallas as pl
from jax.experimental.pallas import tpu as pltpu
from jax.sharding import Mesh, PartitionSpec as P

D = 2048
HEAD = 64
LEV = 2
CLAT = 3
WLON = 12
WIN = 2 * CLAT * LEV * WLON
HALF = WIN // 2
SLOTS = 8
STEP = 2
ROWS = STEP * WIN
TOK = SLOTS * WIN
COLS = 256
HEADS_DEV = COLS // HEAD
SCALE = HEAD ** (-0.5)
BLK = 128
EPSILON = 1e-05
bf16 = jnp.bfloat16
f32 = jnp.float32

ALL = ("zh", "zl", "xh", "lat", "xl", "core")
OUTER = ("zh", "zl", "xh")
ROW = ("zh", "zl", "xh", "lat")
LON = ("xl", "core")
NEAR = ("zl", "xh")


def nn(a, b):
    return lax.dot_general(a, b, (((1,), (0,)), ((), ())), preferred_element_type=f32)


def nt(a, b):
    return lax.dot_general(a, b, (((1,), (1,)), ((), ())), preferred_element_type=f32)


def tn(a, b):
    return lax.dot_general(a, b, (((0,), (0,)), ((), ())), preferred_element_type=f32)


def assemble(pos_ref, pieces, wq_ref, wo_ref):
    for n, piece in enumerate(pieces):
        for c in range(2):
            rows = pl.ds(pl.multiple_of(pos_ref[2 * n + c] * BLK, BLK), BLK)
            for blk in range(2):
                for i in range(3):
                    wq_ref[rows, (2 * i + blk) * BLK : (2 * i + blk + 1) * BLK] = piece[c, blk, i]
                wo_ref[rows, blk * BLK : (blk + 1) * BLK] = piece[c, blk, 3]


def choose(step, own_ref, sib_ref, out_ref):
    @pl.when(step < HALF_STEPS)
    def _():
        out_ref[...] = own_ref[...]

    @pl.when(step >= HALF_STEPS)
    def _():
        out_ref[...] = sib_ref[...]


def forward_kernel(cut_ref, pos_ref, own_ref, sib_ref, *refs):
    pieces, (qkv_ref, att_ref, p_ref, wq_ref, wo_ref, x_ref) = refs[:8], refs[8:]
    step = pl.program_id(0)

    @pl.when(step == 0)
    def _():
        assemble(pos_ref, pieces, wq_ref, wo_ref)

    choose(step, own_ref, sib_ref, x_ref)
    for n in range(3):
        cols = slice(n * COLS, (n + 1) * COLS)
        qkv_ref[:, cols] = nn(x_ref[...], wq_ref[:, cols]).astype(bf16)
    row = lax.broadcasted_iota(jnp.int32, (WIN, WIN), 0) >= HALF
    col = lax.broadcasted_iota(jnp.int32, (WIN, WIN), 1) >= HALF
    same = row == col
    for w in range(STEP):
        rows = slice(w * WIN, (w + 1) * WIN)
        allowed = jnp.logical_or(same, cut_ref[step * STEP + w] == 0)
        for h in range(HEADS_DEV):
            q = qkv_ref[rows, h * HEAD : (h + 1) * HEAD]
            k = qkv_ref[rows, COLS + h * HEAD : COLS + (h + 1) * HEAD]
            v = qkv_ref[rows, 2 * COLS + h * HEAD : 2 * COLS + (h + 1) * HEAD]
            s = jnp.where(allowed, nt(q * bf16(SCALE), k), -1e30)
            e = jnp.exp(s - jnp.max(s, -1, keepdims=True))
            p = e * (1.0 / jnp.sum(e, -1, keepdims=True))
            p_ref[w, h] = p
            att_ref[rows, h * HEAD : (h + 1) * HEAD] = nn(p.astype(bf16), v).astype(bf16)


def backward_kernel(own_ref, sib_ref, qkv_ref, p_ref, wo_ref, _, dp_ref, sent_ref, cot_ref):
    choose(pl.program_id(0), own_ref, sib_ref, cot_ref)
    d_att = nn(cot_ref[...], wo_ref[...]).astype(bf16)
    for w in range(STEP):
        rows = slice(w * WIN, (w + 1) * WIN)
        for h in range(HEADS_DEV):
            q = qkv_ref[rows, h * HEAD : (h + 1) * HEAD]
            k = qkv_ref[rows, COLS + h * HEAD : COLS + (h + 1) * HEAD]
            v = qkv_ref[rows, 2 * COLS + h * HEAD : 2 * COLS + (h + 1) * HEAD]
            p = p_ref[w, h]
            d_o = d_att[rows, h * HEAD : (h + 1) * HEAD]
            d_w = nt(d_o, v)
            dots = jnp.sum(p * d_w, -1, keepdims=True)
            d_s = (p * (d_w - dots) * SCALE).astype(bf16)
            dp_ref[rows, h * HEAD : (h + 1) * HEAD] = nn(d_s, k).astype(bf16)
            dp_ref[rows, COLS + h * HEAD : COLS + (h + 1) * HEAD] = tn(d_s, q).astype(bf16)
            dp_ref[rows, 2 * COLS + h * HEAD : 2 * COLS + (h + 1) * HEAD] = tn(p.astype(bf16), d_o).astype(bf16)

    @pl.when(pl.program_id(0) >= HALF_STEPS)
    def _():
        sent_ref[...] = dp_ref[...]


def grads_kernel(count, where_ref, xa_ref, xb_ref, ca_ref, cb_ref, dp_ref, att_ref, _, *refs):
    step = pl.program_id(0)
    core = where_ref[count]
    g_refs, (x_ref, cot_ref) = refs[:count], refs[count:]
    x_ref[:PART, :], x_ref[PART:, :] = xa_ref[...], xb_ref[...]
    cot_ref[:PART, :], cot_ref[PART:, :] = ca_ref[...], cb_ref[...]
    gq = tn(x_ref[...], dp_ref[...]).astype(bf16)
    go = tn(cot_ref[...], att_ref[...]).astype(bf16)
    for n, g_ref in enumerate(g_refs):

        @pl.when(step == n)
        def _():
            for part in range(2):
                rows = slice(part * BLK, (part + 1) * BLK)
                place = part ^ core
                for blk in range(2):
                    for i in range(3):
                        g_ref[place, blk, i] = gq[rows, (2 * i + blk) * BLK : (2 * i + blk + 1) * BLK]
                    g_ref[place, blk, 3] = go[rows, blk * BLK : (blk + 1) * BLK]


def product(lead, out, pair, slots):
    for n, (ref, at) in enumerate(slots):
        target = pair if ref else lead
        target[at * WIN : (at + 1) * WIN, :] = out[n * WIN : (n + 1) * WIN, :]


def rolled_kernel(dp_ref, in_ref, w_ref, other_ref, x_ref, _, lead_ref, pair_ref, gain_ref):
    total = nt(dp_ref[...], w_ref[...]) + nt(in_ref[...], other_ref[...])
    product(lead_ref, total.astype(bf16), pair_ref, ((0, 0), (0, 1), (1, 0), (1, 1)))
    gain_ref[...] = jnp.sum(total * x_ref[...].astype(f32), 0, keepdims=True)


def branch_kernel(att_ref, w_ref, _, own_ref, sib_ref):
    total = nt(att_ref[...], w_ref[...]).astype(bf16)
    own_ref[...] = total[:PART]
    sib_ref[...] = total[PART:]


def finish_kernel(where_ref, a_ref, b_ref, c_ref, d_ref, gq_ref, go_ref):
    for n, ref in enumerate((a_ref, b_ref, c_ref, d_ref)):
        rows = pl.ds(pl.multiple_of(where_ref[4 + n] * BLK, BLK), BLK)
        for i in range(3):
            gq_ref[i, rows, :] = ref[0, i].astype(f32)
        go_ref[:, rows] = ref[0, 3].astype(f32).T


def params():
    return pltpu.CompilerParams(dimension_semantics=("arbitrary",), vmem_limit_bytes=63 * 1024 * 1024)


PART = TOK // 2
HALF_STEPS = SLOTS // STEP // 2
own_spec = pl.BlockSpec((ROWS, D), lambda i: (jnp.minimum(i, HALF_STEPS - 1), 0))
sib_spec = pl.BlockSpec((ROWS, D), lambda i: (jnp.maximum(i - HALF_STEPS, 0), 0))
p_spec = pl.BlockSpec((STEP, HEADS_DEV, WIN, WIN), lambda i: (i, 0, 0, 0))
smem = pl.BlockSpec(memory_space=pltpu.SMEM)
unread = pl.BlockSpec(memory_space=pl.ANY)
WIDE, STRIP = 1024, 512
strip_column = pl.BlockSpec((PART, STRIP), lambda i: (0, i))
wide_column = pl.BlockSpec((PART, WIDE), lambda i: (0, i))


def rows_spec(cols):
    return pl.BlockSpec((ROWS, cols), lambda i: (i, 0))


def later_spec(cols):
    return pl.BlockSpec((ROWS, cols), lambda i: (jnp.maximum(i - HALF_STEPS, 0), 0))


def whole(*shape):
    return pl.BlockSpec(shape, lambda *i: (0,) * len(shape))


def shaped(shape, dtype=bf16):
    return jax.ShapeDtypeStruct(shape, dtype)


def forward(cut, pos, own, sib, weights):
    return pl.pallas_call(
        forward_kernel,
        grid=(SLOTS // STEP,),
        in_specs=[smem, smem, own_spec, sib_spec] + [whole(*w.shape) for w in weights],
        out_specs=[
            rows_spec(3 * COLS),
            rows_spec(COLS),
            p_spec,
            whole(D, 3 * COLS),
            whole(D, COLS),
        ],
        out_shape=[
            shaped((TOK, 3 * COLS)),
            shaped((TOK, COLS)),
            shaped((SLOTS, HEADS_DEV, WIN, WIN), f32),
            shaped((D, 3 * COLS)),
            shaped((D, COLS)),
        ],
        scratch_shapes=[pltpu.VMEM((ROWS, D), bf16)],
        compiler_params=params(),
        name="attention_forward",
    )(cut, pos, own, sib, *weights)


def backward(own, sib, qkv, p, wo, before):
    return pl.pallas_call(
        backward_kernel,
        grid=(SLOTS // STEP,),
        in_specs=[own_spec, sib_spec, rows_spec(3 * COLS), p_spec, whole(D, COLS), unread],
        out_specs=[rows_spec(3 * COLS), later_spec(3 * COLS)],
        out_shape=[shaped((TOK, 3 * COLS)), shaped((PART, 3 * COLS))],
        scratch_shapes=[pltpu.VMEM((ROWS, D), bf16)],
        compiler_params=params(),
        name="attention_backward",
    )(own, sib, qkv, p, wo, before)


def grads(chips, core, xs, cots, dp, att, before):
    count = len(chips)
    part = pl.BlockSpec((PART, 2 * BLK), lambda i, where: (0, where[i]))
    return pl.pallas_call(
        functools.partial(grads_kernel, count),
        grid_spec=pltpu.PrefetchScalarGridSpec(
            num_scalar_prefetch=1,
            grid=(count,),
            in_specs=[part] * 4 + [whole(TOK, 3 * COLS), whole(TOK, COLS), unread],
            out_specs=[whole(2, 2, 4, BLK, BLK)] * count,
            scratch_shapes=[pltpu.VMEM((TOK, 2 * BLK), bf16)] * 2,
        ),
        out_shape=[shaped((2, 2, 4, BLK, BLK))] * count,
        compiler_params=params(),
        name="weight_gradients",
    )(jnp.stack(list(chips) + [core]), *xs, *cots, dp, att, before)


def rolled_gradient(dp, dp_in, wq, wq_in, x, before):
    depth = 3 * COLS
    strip = pl.BlockSpec((STRIP, depth), lambda i: (i, 0))
    half = pl.BlockSpec((PART // 2, STRIP), lambda i: (0, i))
    return pl.pallas_call(
        rolled_kernel,
        grid=(D // STRIP,),
        in_specs=[whole(PART, depth)] * 2 + [strip] * 2 + [strip_column, unread],
        out_specs=[half, half, pl.BlockSpec((1, STRIP), lambda i: (0, i))],
        out_shape=[shaped((PART // 2, D))] * 2 + [shaped((1, D), f32)],
        compiler_params=params(),
        name="rolled_gradient",
    )(dp, dp_in, wq, wq_in, x, before)


def branch_product(att, wo, before):
    return pl.pallas_call(
        branch_kernel,
        grid=(D // WIDE,),
        in_specs=[whole(TOK, COLS), pl.BlockSpec((WIDE, COLS), lambda i: (i, 0)), unread],
        out_specs=[wide_column, wide_column],
        out_shape=[shaped((PART, D))] * 2,
        compiler_params=params(),
        name="branch_product",
    )(att, wo, before)


def finish(where, parts):
    return pl.pallas_call(
        finish_kernel,
        grid_spec=pltpu.PrefetchScalarGridSpec(
            num_scalar_prefetch=1,
            grid=(4,),
            in_specs=[pl.BlockSpec((1, 4, BLK, BLK), lambda s, where: (s, 0, 0, 0))] * 4,
            out_specs=[
                pl.BlockSpec((3, 4 * BLK, BLK), lambda s, where: (0, where[s], 0)),
                pl.BlockSpec((BLK, 4 * BLK), lambda s, where: (0, where[s])),
            ],
        ),
        out_shape=[shaped((3, D, BLK), f32), shaped((BLK, D), f32)],
        compiler_params=params(),
        name="finish_gradients",
    )(where, *parts)


def small(body, ins, outs, before=(), specs=(), scratch=(), name=None):
    specs = dict(specs)
    in_specs = [specs.get(n, whole(*x.shape)) for n, x in enumerate(ins)] + [unread] * len(before)
    count, extra = len(ins), len(before)

    def kernel(*refs):
        body(*refs[:count], *refs[count + extra :])

    return pl.pallas_call(
        kernel,
        grid=(1,),
        in_specs=in_specs,
        out_specs=[whole(*x.shape) for x in outs],
        out_shape=list(outs),
        scratch_shapes=list(scratch),
        compiler_params=params(),
        name=name,
    )(*ins, *before)


QUARTER = WIN // 4
UNIT = (4, BLK, BLK)
PAIR = (2,) + UNIT
FOUR = (2, 2) + UNIT
GAIN = (16, BLK)


def wide(*refs):
    total = refs[0].astype(f32)
    for ref in refs[1:]:
        total = total + ref.astype(f32)
    return total


def add_low(*values):
    return wide(*values).astype(bf16)


def select_body(half_ref, u0, u1, u2, u3, keep, give):
    @pl.when(half_ref[0] == 0)
    def _():
        keep[0], keep[1], give[0], give[1] = u0[...], u1[...], u2[...], u3[...]

    @pl.when(half_ref[0] != 0)
    def _():
        keep[0], keep[1], give[0], give[1] = u2[...], u3[...], u0[...], u1[...]


def join_body(*refs):
    out = refs[-1]
    for n, ref in enumerate(refs[:-1]):
        out[n] = ref[...]


def rows_body(*refs):
    out = refs[-1]
    for n, ref in enumerate(refs[:-1]):
        out[n * WIN : (n + 1) * WIN, :] = ref[...]


def pin_body(out):
    out[...] = jnp.zeros_like(out)


def normal(values):
    centered = values - jnp.mean(values, -1, keepdims=True)
    inverse_std = lax.rsqrt(jnp.mean(centered * centered, -1, keepdims=True) + EPSILON)
    return centered * inverse_std, inverse_std


def enter_body(own, right, below, corner, gain, rolled, cot, normed, buffer):
    for n, out in enumerate((rolled, cot)):
        for k, piece in enumerate((own, right, below, corner)):
            buffer[k * QUARTER : (k + 1) * QUARTER, :] = piece[n].astype(f32)
        out[...] = buffer[...].astype(bf16)
        if n == 0:
            normed[...] = (normal(buffer[...])[0] * gain[...]).astype(bf16)


def leave_body(rolled, cot, gain, b0, b1, b2, d0, d1, d2, own, right, below, corner, buffer):
    branch = add_low(b0[...], b1[...], b2[...])
    buffer[...] = rolled[...].astype(f32) + branch.astype(f32)
    for k, piece in enumerate((own, right, below, corner)):
        piece[0] = buffer[k * QUARTER : (k + 1) * QUARTER, :].astype(bf16)
    standard, inverse_std = normal(rolled[...].astype(f32))
    scaled = add_low(d0[...], d1[...], d2[...]).astype(f32) * gain[...]
    local = inverse_std * (
        scaled
        - jnp.mean(scaled, -1, keepdims=True)
        - standard * jnp.mean(scaled * standard, -1, keepdims=True)
    )
    buffer[...] = cot[...].astype(f32) + local
    for k, piece in enumerate((own, right, below, corner)):
        piece[1] = buffer[k * QUARTER : (k + 1) * QUARTER, :].astype(bf16)


def windows_body(own, other, lead, pair):
    for n, (out, at) in enumerate(((lead, 0), (pair, 0), (lead, 1), (pair, 1))):
        rows = slice(n * WIN, (n + 1) * WIN)
        out[at * WIN : (at + 1) * WIN, :] = add_low(own[rows, :], other[rows, :])


def mid_body(lead, given, out):
    out[...] = add_low(lead[...], given[...])


def gain_mid_body(lead, given, gain, gain_in, out, gain_out):
    mid_body(lead, given, out)
    gain_out[...] = gain[...] + gain_in[...]


def sides_body(g10, g11, g30, g31, back1, back3, to1, to3):
    to1[0], to1[1] = g10[...], add_low(g11[...], back1[...])
    to3[0], to3[1] = add_low(g30[...], back3[...]), g31[...]


def lat_body(g00, g01, in1, in3, gain, gain_in, t0, t1, gain_out):
    t0[...] = add_low(g00[...], in1[0], in3[0])
    t1[...] = add_low(g01[...], in1[1], in3[1])
    gain_out[...] = gain[...] + gain_in[...]


def xl_body(t0, crossing, gain, gain_in, ours, others, gain_out):
    ours[...] = add_low(t0[0], crossing[0])
    others[...] = add_low(t0[1], crossing[1])
    gain_out[...] = gain[...] + gain_in[...]


def core_body(half_ref, ours, theirs, gain, gain_in, s0, s1, s2, s3, gain_out):
    gain_out[...] = gain[...] + gain_in[...]

    @pl.when(half_ref[0] == 0)
    def _():
        s0[...], s1[...], s2[...], s3[...] = ours[0], ours[1], theirs[0], theirs[1]

    @pl.when(half_ref[0] != 0)
    def _():
        s0[...], s1[...], s2[...], s3[...] = theirs[0], theirs[1], ours[0], ours[1]


def zh_body(kept, b1, b2, b3, gains, unit, total):
    unit[...] = add_low(kept[...], b1[...], b2[...], b3[...])
    total[...] = jnp.sum(gains[...], 0)


def shift(x, axes, by):
    count = lax.axis_size(axes)
    return lax.ppermute(x, axes, [(i, (i + by) % count) for i in range(count)])


def swap(x, axes, mask):
    count = lax.axis_size(axes)
    return lax.ppermute(x, axes, [(i, i ^ mask) for i in range(count)])


def shift_both(x, by):
    rows, cols = lax.axis_size(ROW), lax.axis_size(LON)
    pairs = [
        (r * cols + c, (r + by) % rows * cols + (c + by) % cols)
        for r in range(rows)
        for c in range(cols)
    ]
    return lax.ppermute(x, ALL, pairs)


def quarters(*arrays):
    arrays = [x.transpose(0, 2, 1, 3) for x in arrays]
    lon = WLON // 2

    def cut(rows, cols):
        return jnp.stack([x[rows, cols].reshape(QUARTER, D) for x in arrays])

    first, last = slice(0, CLAT), slice(CLAT, 2 * CLAT)
    west, east = slice(0, lon), slice(lon, WLON)
    below = shift(cut(first, east), ROW, -1)
    corner = shift_both(cut(first, west), -1)
    right = shift(cut(last, west), LON, -1)
    return cut(last, east), right, below, corner


def back_home(before, own, right, below, corner):
    below, corner, right = shift(below, ROW, 1), shift_both(corner, 1), shift(right, LON, 1)
    below, corner, right, _ = lax.optimization_barrier((below, corner, right, before))
    own, right, below, corner = (
        x.reshape(2, CLAT, WLON // 2, LEV, D) for x in (own, right, below, corner)
    )
    top = jnp.concatenate([corner, below], axis=2)
    bottom = jnp.concatenate([right, own], axis=2)
    both = jnp.concatenate([top, bottom], axis=1).transpose(0, 1, 3, 2, 4)
    return both[0], both[1]


def weight_unit(w_qkv, w_out, place):
    qkv = lax.dynamic_slice(w_qkv.transpose(1, 0, 2), (0, place * BLK, 0), (3, BLK, BLK))
    out = lax.dynamic_slice(w_out, (0, place * BLK), (BLK, BLK)).T
    return jnp.concatenate([qkv, out[None]], axis=0)


def shards(tokens, norm_gain, w_qkv, w_out, grad_out):
    zh, lat, xl, core = (lax.axis_index(a) for a in ("zh", "lat", "xl", "core"))
    half = ((zh // 2) ^ core).reshape(1)
    chips = {(s, t): (lat ^ s) * 2 + (xl ^ t) for s in range(4) for t in range(2)}
    pos = jnp.stack([chips[place] * 2 + (core ^ c) for place in sorted(chips) for c in range(2)])
    ends = jnp.stack(
        [lat ^ s for s in range(4)] + [(xl ^ t) * 2 + (core ^ c) for c in range(2) for t in range(2)]
    )
    edge = jnp.logical_and(zh == 3, lat == 3)
    owners = lax.axis_index(NEAR) ^ (jnp.arange(SLOTS) % 4)
    cut = jnp.logical_and(edge, owners == 3).astype(jnp.int32)
    gain_row = norm_gain.reshape(1, D)
    token = shaped((8, BLK), f32)
    window, windows = shaped((WIN, D)), shaped((4 * WIN, D))
    scalar = {0: smem}

    unit = weight_unit(w_qkv, w_out, pos[0])
    units = [unit] + [swap(unit, "zh", s) for s in (1, 2, 3)]
    pieces = quarters(tokens, grad_out)
    keep, give = small(select_body, [half] + units, [shaped(PAIR)] * 2, specs=scalar, name="select")
    given = swap(give, "core", 1)
    buffer = [pltpu.VMEM((WIN, D), f32)]
    rolled, cotangent, normed = small(
        enter_body, [*pieces, gain_row], [window] * 3, before=[give], scratch=buffer, name="enter"
    )
    (mine,) = small(join_body, [keep, given], [shaped(FOUR)], before=[normed], name="join")
    near = swap(mine, "xl", 1)
    m1a, m3a = swap(mine, "lat", 1), swap(mine, "lat", 3)
    x1, x2 = swap(normed, NEAR, 1), swap(normed, NEAR, 2)
    (pin,) = small(pin_body, [], [token], before=[near, m1a, m3a], name="pin")
    m1b, m3b = swap(near, "lat", 1), swap(near, "lat", 3)
    o0 = swap(m1a, "lat", 3)
    (pin,) = small(pin_body, [], [token], before=[m1b, m3b, x1, x2, pin], name="pin")
    o1 = swap(m3b, "lat", 1)
    x3 = swap(lax.optimization_barrier((x1, pin))[0], NEAR, 2)
    (x_own,) = small(rows_body, [normed, x1, x2, x3], [windows], before=[o0, o1, pin], name="rows")
    x_sib = swap(x_own, "core", 1)
    c1, c2, c3 = (swap(cotangent, NEAR, s) for s in (1, 2, 3))

    weights = [mine, near, m1a, m1b, o0, o1, m3a, m3b]
    qkv, att, p, wq, wo = forward(cut, pos, x_own, x_sib, weights)
    (c_own,) = small(rows_body, [cotangent, c1, c2, c3], [windows], before=[wo], name="rows")
    c_sib = swap(c_own, "core", 1)
    b_own, b_sib = branch_product(att, wo, c_own)
    b_other = swap(b_sib, "core", 1)
    wq_in = swap(lax.optimization_barrier((wq, b_own))[0], "core", 1)
    dp, dp_sent = backward(c_own, c_sib, qkv, p, wo, b_own)
    dp_in = swap(dp_sent, "core", 1)
    xs, cots = (x_own, x_sib), (c_own, c_sib)

    far0, far1 = grads([chips[2, 0], chips[2, 1]], core, xs, cots, dp, att, dp)
    back3, back1 = swap(far0, "lat", 1), swap(far1, "lat", 3)
    near_chips = [chips[s, t] for s in (1, 3, 0) for t in range(2)]
    g10, g11, g30, g31, g00, g01 = grads(near_chips, core, xs, cots, dp, att, far0)
    to1, to3 = small(
        sides_body, [g10, g11, g30, g31, back1, back3], [shaped((2,) + FOUR)] * 2, name="sides"
    )
    in1, in3 = swap(to1, "lat", 1), swap(to3, "lat", 3)
    first, second = pl.BlockSpec((WIN, D), lambda i: (0, 0)), pl.BlockSpec((WIN, D), lambda i: (1, 0))
    pair = shaped((2 * WIN, D))
    b_lead, b_pair = small(windows_body, [b_own, b_other], [pair] * 2, before=[to1], name="windows")
    b_in = swap(b_pair, NEAR, 1)
    d_lead, d_pair, gain = rolled_gradient(dp, dp_in, wq, wq_in, x_own, b_pair)
    d_in = swap(d_pair, NEAR, 2)

    gain, gain_shape = gain.reshape(GAIN), shaped(GAIN, f32)
    gain_in = swap(gain, ALL, 1)
    t0, t1, gain = small(
        lat_body,
        [g00, g01, in1, in3, gain, gain_in],
        [shaped(FOUR), shaped(FOUR), gain_shape],
        name="lat_sum",
    )
    crossing, gain_in = swap(t1, "xl", 1), swap(gain, ALL, 4)
    b_mid, gain = small(
        gain_mid_body,
        [b_lead, b_in, gain, gain_in],
        [window, gain_shape],
        before=[t1],
        specs={0: second, 1: second},
        name="mid",
    )
    b_last, gain_in = swap(b_mid, NEAR, 2), swap(gain, ALL, 2)
    ours, others, gain = small(
        xl_body,
        [t0, crossing, gain, gain_in],
        [shaped(PAIR)] * 2 + [gain_shape],
        before=[b_mid],
        name="xl_sum",
    )
    theirs, gain_in = swap(others, "core", 1), swap(gain, ALL, 8)
    (d_mid,) = small(
        mid_body, [d_lead, d_in], [window], before=[ours], specs={0: second, 1: second}, name="mid"
    )
    d_last = swap(d_mid, NEAR, 1)
    *sent, gain = small(
        core_body,
        [half, ours, theirs, gain, gain_in],
        [shaped(UNIT)] * 4 + [gain_shape],
        before=[d_mid],
        specs=scalar,
        name="core_sum",
    )
    back = [swap(sent[s], "zh", s) for s in (1, 2, 3)]
    gains = lax.all_gather(gain, OUTER, axis=0)
    unit, gain = small(
        zh_body, [sent[0], *back, gains], [shaped(UNIT), gain_shape], before=[b_last], name="zh_sum"
    )
    around = [swap(unit, "lat", s) for s in (1, 2, 3)]
    results = small(
        leave_body,
        [rolled, cotangent, gain_row, b_lead, b_in, b_last, d_lead, d_in, d_last],
        [shaped((2, QUARTER, D))] * 4,
        before=[unit],
        specs={n: first for n in (3, 4, 6, 7)},
        scratch=buffer,
        name="leave",
    )
    (rows,) = small(
        join_body, [unit, *around], [shaped((4,) + UNIT)], before=[results[0]], name="slices"
    )
    near_rows, core_rows = swap(rows, "xl", 1), swap(rows, "core", 1)
    results, _ = lax.optimization_barrier((results, rows))
    output, grad_tokens = back_home(rows, *results)
    near_rows, output, _ = lax.optimization_barrier((near_rows, output, grad_tokens))
    last_rows = swap(near_rows, "core", 1)
    grad_wqkv, grad_wout = finish(ends, [rows, near_rows, core_rows, last_rows])
    grad_gain = gain.reshape(D) / norm_gain
    return output, grad_tokens, grad_wqkv.transpose(1, 0, 2), grad_wout, grad_gain


def solution(mesh):
    fine = Mesh(mesh.devices.reshape(4, 2, 2, 4, 2, 2), ALL)
    by_token = P(ROW, None, LON, None)
    in_specs = (by_token, P(), P(None, None, OUTER), P(OUTER, None), by_token)
    out_specs = (by_token, by_token, P(None, None, OUTER), P(OUTER, None), P())
    return jax.shard_map(shards, mesh=fine, in_specs=in_specs, out_specs=out_specs, check_vma=False)
```

```python
import functools

import jax
import jax.numpy as jnp
from jax import lax
from jax.experimental import pallas as pl
from jax.experimental.pallas import tpu as pltpu
from jax.sharding import Mesh, PartitionSpec as P

D = 2048
HEAD = 64
LEV = 2
CLAT = 3
WLON = 12
WIN = 2 * CLAT * LEV * WLON
HALF = WIN // 2
SLOTS = 8
STEP = 2
ROWS = STEP * WIN
TOK = SLOTS * WIN
COLS = 256
HEADS_DEV = COLS // HEAD
SCALE = HEAD ** (-0.5)
BLK = 128
EPSILON = 1e-05
bf16 = jnp.bfloat16
f32 = jnp.float32

ALL = ("zh", "zl", "xh", "lat", "xl", "core")
OUTER = ("zh", "zl", "xh")
ROW = ("zh", "zl", "xh", "lat")
LON = ("xl", "core")
NEAR = ("zl", "xh")


def nn(a, b):
    return lax.dot_general(a, b, (((1,), (0,)), ((), ())), preferred_element_type=f32)


def nt(a, b):
    return lax.dot_general(a, b, (((1,), (1,)), ((), ())), preferred_element_type=f32)


def tn(a, b):
    return lax.dot_general(a, b, (((0,), (0,)), ((), ())), preferred_element_type=f32)


def assemble(pos_ref, pieces, wq_ref, wo_ref):
    for n, piece in enumerate(pieces):
        for c in range(2):
            rows = pl.ds(pl.multiple_of(pos_ref[2 * n + c] * BLK, BLK), BLK)
            for blk in range(2):
                for i in range(3):
                    wq_ref[rows, (2 * i + blk) * BLK : (2 * i + blk + 1) * BLK] = piece[c, blk, i]
                wo_ref[rows, blk * BLK : (blk + 1) * BLK] = piece[c, blk, 3]


def choose(step, own_ref, sib_ref, out_ref):
    @pl.when(step < HALF_STEPS)
    def _():
        out_ref[...] = own_ref[...]

    @pl.when(step >= HALF_STEPS)
    def _():
        out_ref[...] = sib_ref[...]


def forward_kernel(cut_ref, pos_ref, own_ref, sib_ref, *refs):
    pieces, (qkv_ref, att_ref, p_ref, wq_ref, wo_ref, x_ref) = refs[:8], refs[8:]
    step = pl.program_id(0)

    @pl.when(step == 0)
    def _():
        assemble(pos_ref, pieces, wq_ref, wo_ref)

    choose(step, own_ref, sib_ref, x_ref)
    for n in range(3):
        cols = slice(n * COLS, (n + 1) * COLS)
        qkv_ref[:, cols] = nn(x_ref[...], wq_ref[:, cols]).astype(bf16)
    row = lax.broadcasted_iota(jnp.int32, (WIN, WIN), 0) >= HALF
    col = lax.broadcasted_iota(jnp.int32, (WIN, WIN), 1) >= HALF
    same = row == col
    for w in range(STEP):
        rows = slice(w * WIN, (w + 1) * WIN)
        allowed = jnp.logical_or(same, cut_ref[step * STEP + w] == 0)
        for h in range(HEADS_DEV):
            q = qkv_ref[rows, h * HEAD : (h + 1) * HEAD]
            k = qkv_ref[rows, COLS + h * HEAD : COLS + (h + 1) * HEAD]
            v = qkv_ref[rows, 2 * COLS + h * HEAD : 2 * COLS + (h + 1) * HEAD]
            s = jnp.where(allowed, nt(q * bf16(SCALE), k), -1e30)
            e = jnp.exp(s - jnp.max(s, -1, keepdims=True))
            p = e * (1.0 / jnp.sum(e, -1, keepdims=True))
            p_ref[w, h] = p
            att_ref[rows, h * HEAD : (h + 1) * HEAD] = nn(p.astype(bf16), v).astype(bf16)


def backward_kernel(own_ref, sib_ref, qkv_ref, p_ref, wo_ref, _, dp_ref, sent_ref, cot_ref):
    choose(pl.program_id(0), own_ref, sib_ref, cot_ref)
    d_att = nn(cot_ref[...], wo_ref[...]).astype(bf16)
    for w in range(STEP):
        rows = slice(w * WIN, (w + 1) * WIN)
        for h in range(HEADS_DEV):
            q = qkv_ref[rows, h * HEAD : (h + 1) * HEAD]
            k = qkv_ref[rows, COLS + h * HEAD : COLS + (h + 1) * HEAD]
            v = qkv_ref[rows, 2 * COLS + h * HEAD : 2 * COLS + (h + 1) * HEAD]
            p = p_ref[w, h]
            d_o = d_att[rows, h * HEAD : (h + 1) * HEAD]
            d_w = nt(d_o, v)
            dots = jnp.sum(p * d_w, -1, keepdims=True)
            d_s = (p * (d_w - dots) * SCALE).astype(bf16)
            dp_ref[rows, h * HEAD : (h + 1) * HEAD] = nn(d_s, k).astype(bf16)
            dp_ref[rows, COLS + h * HEAD : COLS + (h + 1) * HEAD] = tn(d_s, q).astype(bf16)
            dp_ref[rows, 2 * COLS + h * HEAD : 2 * COLS + (h + 1) * HEAD] = tn(p.astype(bf16), d_o).astype(bf16)

    @pl.when(pl.program_id(0) >= HALF_STEPS)
    def _():
        sent_ref[...] = dp_ref[...]


def grads_kernel(count, where_ref, xa_ref, xb_ref, ca_ref, cb_ref, dp_ref, att_ref, _, *refs):
    step = pl.program_id(0)
    core = where_ref[count]
    g_refs, (x_ref, cot_ref) = refs[:count], refs[count:]
    x_ref[:PART, :], x_ref[PART:, :] = xa_ref[...], xb_ref[...]
    cot_ref[:PART, :], cot_ref[PART:, :] = ca_ref[...], cb_ref[...]
    gq = tn(x_ref[...], dp_ref[...]).astype(bf16)
    go = tn(cot_ref[...], att_ref[...]).astype(bf16)
    for n, g_ref in enumerate(g_refs):

        @pl.when(step == n)
        def _():
            for part in range(2):
                rows = slice(part * BLK, (part + 1) * BLK)
                place = part ^ core
                for blk in range(2):
                    for i in range(3):
                        g_ref[place, blk, i] = gq[rows, (2 * i + blk) * BLK : (2 * i + blk + 1) * BLK]
                    g_ref[place, blk, 3] = go[rows, blk * BLK : (blk + 1) * BLK]


def product(lead, out, pair, slots):
    for n, (ref, at) in enumerate(slots):
        target = pair if ref else lead
        target[at * WIN : (at + 1) * WIN, :] = out[n * WIN : (n + 1) * WIN, :]


def rolled_kernel(dp_ref, in_ref, w_ref, other_ref, x_ref, _, lead_ref, pair_ref, gain_ref):
    total = nt(dp_ref[...], w_ref[...]) + nt(in_ref[...], other_ref[...])
    product(lead_ref, total.astype(bf16), pair_ref, ((0, 0), (0, 1), (1, 0), (1, 1)))
    gain_ref[...] = jnp.sum(total * x_ref[...].astype(f32), 0, keepdims=True)


def branch_kernel(att_ref, w_ref, _, own_ref, sib_ref):
    total = nt(att_ref[...], w_ref[...]).astype(bf16)
    own_ref[...] = total[:PART]
    sib_ref[...] = total[PART:]


def finish_kernel(where_ref, a_ref, b_ref, c_ref, d_ref, gain, gain_in, gq_ref, go_ref, gain_out):
    gain_out[...] = gain[...] + gain_in[...]
    for n, ref in enumerate((a_ref, b_ref, c_ref, d_ref)):
        rows = pl.ds(pl.multiple_of(where_ref[4 + n] * BLK, BLK), BLK)
        for i in range(3):
            gq_ref[i, rows, :] = ref[0, i].astype(f32)
        go_ref[:, rows] = ref[0, 3].astype(f32).T


def params():
    return pltpu.CompilerParams(dimension_semantics=("arbitrary",), vmem_limit_bytes=63 * 1024 * 1024)


PART = TOK // 2
HALF_STEPS = SLOTS // STEP // 2
own_spec = pl.BlockSpec((ROWS, D), lambda i: (jnp.minimum(i, HALF_STEPS - 1), 0))
sib_spec = pl.BlockSpec((ROWS, D), lambda i: (jnp.maximum(i - HALF_STEPS, 0), 0))
p_spec = pl.BlockSpec((STEP, HEADS_DEV, WIN, WIN), lambda i: (i, 0, 0, 0))
smem = pl.BlockSpec(memory_space=pltpu.SMEM)
unread = pl.BlockSpec(memory_space=pl.ANY)
WIDE, STRIP = 1024, 512
strip_column = pl.BlockSpec((PART, STRIP), lambda i: (0, i))
wide_column = pl.BlockSpec((PART, WIDE), lambda i: (0, i))


def rows_spec(cols):
    return pl.BlockSpec((ROWS, cols), lambda i: (i, 0))


def later_spec(cols):
    return pl.BlockSpec((ROWS, cols), lambda i: (jnp.maximum(i - HALF_STEPS, 0), 0))


def whole(*shape):
    return pl.BlockSpec(shape, lambda *i: (0,) * len(shape))


def shaped(shape, dtype=bf16):
    return jax.ShapeDtypeStruct(shape, dtype)


def forward(cut, pos, own, sib, weights):
    return pl.pallas_call(
        forward_kernel,
        grid=(SLOTS // STEP,),
        in_specs=[smem, smem, own_spec, sib_spec] + [whole(*w.shape) for w in weights],
        out_specs=[
            rows_spec(3 * COLS),
            rows_spec(COLS),
            p_spec,
            whole(D, 3 * COLS),
            whole(D, COLS),
        ],
        out_shape=[
            shaped((TOK, 3 * COLS)),
            shaped((TOK, COLS)),
            shaped((SLOTS, HEADS_DEV, WIN, WIN), f32),
            shaped((D, 3 * COLS)),
            shaped((D, COLS)),
        ],
        scratch_shapes=[pltpu.VMEM((ROWS, D), bf16)],
        compiler_params=params(),
        name="attention_forward",
    )(cut, pos, own, sib, *weights)


def backward(own, sib, qkv, p, wo, before):
    return pl.pallas_call(
        backward_kernel,
        grid=(SLOTS // STEP,),
        in_specs=[own_spec, sib_spec, rows_spec(3 * COLS), p_spec, whole(D, COLS), unread],
        out_specs=[rows_spec(3 * COLS), later_spec(3 * COLS)],
        out_shape=[shaped((TOK, 3 * COLS)), shaped((PART, 3 * COLS))],
        scratch_shapes=[pltpu.VMEM((ROWS, D), bf16)],
        compiler_params=params(),
        name="attention_backward",
    )(own, sib, qkv, p, wo, before)


def grads(chips, core, xs, cots, dp, att, before):
    count = len(chips)
    part = pl.BlockSpec((PART, 2 * BLK), lambda i, where: (0, where[i]))
    return pl.pallas_call(
        functools.partial(grads_kernel, count),
        grid_spec=pltpu.PrefetchScalarGridSpec(
            num_scalar_prefetch=1,
            grid=(count,),
            in_specs=[part] * 4 + [whole(TOK, 3 * COLS), whole(TOK, COLS), unread],
            out_specs=[whole(2, 2, 4, BLK, BLK)] * count,
            scratch_shapes=[pltpu.VMEM((TOK, 2 * BLK), bf16)] * 2,
        ),
        out_shape=[shaped((2, 2, 4, BLK, BLK))] * count,
        compiler_params=params(),
        name="weight_gradients",
    )(jnp.stack(list(chips) + [core]), *xs, *cots, dp, att, before)


def rolled_gradient(dp, dp_in, wq, wq_in, x, before):
    depth = 3 * COLS
    strip = pl.BlockSpec((STRIP, depth), lambda i: (i, 0))
    half = pl.BlockSpec((PART // 2, STRIP), lambda i: (0, i))
    return pl.pallas_call(
        rolled_kernel,
        grid=(D // STRIP,),
        in_specs=[whole(PART, depth)] * 2 + [strip] * 2 + [strip_column, unread],
        out_specs=[half, half, pl.BlockSpec((1, STRIP), lambda i: (0, i))],
        out_shape=[shaped((PART // 2, D))] * 2 + [shaped((1, D), f32)],
        compiler_params=params(),
        name="rolled_gradient",
    )(dp, dp_in, wq, wq_in, x, before)


def branch_product(att, wo, before):
    return pl.pallas_call(
        branch_kernel,
        grid=(D // WIDE,),
        in_specs=[whole(TOK, COLS), pl.BlockSpec((WIDE, COLS), lambda i: (i, 0)), unread],
        out_specs=[wide_column, wide_column],
        out_shape=[shaped((PART, D))] * 2,
        compiler_params=params(),
        name="branch_product",
    )(att, wo, before)


def finish(where, parts, gain, gain_in):
    return pl.pallas_call(
        finish_kernel,
        grid_spec=pltpu.PrefetchScalarGridSpec(
            num_scalar_prefetch=1,
            grid=(4,),
            in_specs=[pl.BlockSpec((1, 4, BLK, BLK), lambda s, where: (s, 0, 0, 0))] * 4 + [whole(16, BLK)] * 2,
            out_specs=[
                pl.BlockSpec((3, 4 * BLK, BLK), lambda s, where: (0, where[s], 0)),
                pl.BlockSpec((BLK, 4 * BLK), lambda s, where: (0, where[s])),
                whole(16, BLK),
            ],
        ),
        out_shape=[shaped((3, D, BLK), f32), shaped((BLK, D), f32), shaped((16, BLK), f32)],
        compiler_params=params(),
        name="finish_gradients",
    )(where, *parts, gain, gain_in)


def small(body, ins, outs, before=(), specs=(), scratch=(), name=None):
    specs = dict(specs)
    in_specs = [specs.get(n, whole(*x.shape)) for n, x in enumerate(ins)] + [unread] * len(before)
    count, extra = len(ins), len(before)

    def kernel(*refs):
        body(*refs[:count], *refs[count + extra :])

    return pl.pallas_call(
        kernel,
        grid=(1,),
        in_specs=in_specs,
        out_specs=[whole(*x.shape) for x in outs],
        out_shape=list(outs),
        scratch_shapes=list(scratch),
        compiler_params=params(),
        name=name,
    )(*ins, *before)


QUARTER = WIN // 4
UNIT = (4, BLK, BLK)
PAIR = (2,) + UNIT
FOUR = (2, 2) + UNIT
GAIN = (16, BLK)


def wide(*refs):
    total = refs[0].astype(f32)
    for ref in refs[1:]:
        total = total + ref.astype(f32)
    return total


def add_low(*values):
    return wide(*values).astype(bf16)


def select_body(half_ref, u0, u1, u2, u3, keep, give):
    @pl.when(half_ref[0] == 0)
    def _():
        keep[0], keep[1], give[0], give[1] = u0[...], u1[...], u2[...], u3[...]

    @pl.when(half_ref[0] != 0)
    def _():
        keep[0], keep[1], give[0], give[1] = u2[...], u3[...], u0[...], u1[...]


def join_body(*refs):
    out = refs[-1]
    for n, ref in enumerate(refs[:-1]):
        out[n] = ref[...]


def rows_body(*refs):
    out = refs[-1]
    for n, ref in enumerate(refs[:-1]):
        out[n * WIN : (n + 1) * WIN, :] = ref[...]


def pin_body(out):
    out[...] = jnp.zeros_like(out)


def normal(values):
    centered = values - jnp.mean(values, -1, keepdims=True)
    inverse_std = lax.rsqrt(jnp.mean(centered * centered, -1, keepdims=True) + EPSILON)
    return centered * inverse_std, inverse_std


def enter_body(own, right, below, corner, gain, rolled, cot, normed, buffer):
    for n, out in enumerate((rolled, cot)):
        for k, piece in enumerate((own, right, below, corner)):
            buffer[k * QUARTER : (k + 1) * QUARTER, :] = piece[n].astype(f32)
        out[...] = buffer[...].astype(bf16)
        if n == 0:
            normed[...] = (normal(buffer[...])[0] * gain[...]).astype(bf16)


def leave_body(rolled, cot, gain, b0, b1, b2, d0, d1, d2, own, right, below, corner, buffer):
    branch = add_low(b0[...], b1[...], b2[...])
    buffer[...] = rolled[...].astype(f32) + branch.astype(f32)
    for k, piece in enumerate((own, right, below, corner)):
        piece[0] = buffer[k * QUARTER : (k + 1) * QUARTER, :].astype(bf16)
    standard, inverse_std = normal(rolled[...].astype(f32))
    scaled = add_low(d0[...], d1[...], d2[...]).astype(f32) * gain[...]
    local = inverse_std * (
        scaled
        - jnp.mean(scaled, -1, keepdims=True)
        - standard * jnp.mean(scaled * standard, -1, keepdims=True)
    )
    buffer[...] = cot[...].astype(f32) + local
    for k, piece in enumerate((own, right, below, corner)):
        piece[1] = buffer[k * QUARTER : (k + 1) * QUARTER, :].astype(bf16)


def windows_body(own, other, lead, pair):
    for n, (out, at) in enumerate(((lead, 0), (pair, 0), (lead, 1), (pair, 1))):
        rows = slice(n * WIN, (n + 1) * WIN)
        out[at * WIN : (at + 1) * WIN, :] = add_low(own[rows, :], other[rows, :])


def mid_body(lead, given, out):
    out[...] = add_low(lead[...], given[...])


def gain_mid_body(lead, given, gain, gain_in, out, gain_out):
    mid_body(lead, given, out)
    gain_out[...] = gain[...] + gain_in[...]


def sides_body(g10, g11, g30, g31, back1, back3, to1, to3):
    to1[0], to1[1] = g10[...], add_low(g11[...], back1[...])
    to3[0], to3[1] = add_low(g30[...], back3[...]), g31[...]


def lat_body(g00, g01, in1, in3, gain, gain_in, t0, t1, gain_out):
    t0[...] = add_low(g00[...], in1[0], in3[0])
    t1[...] = add_low(g01[...], in1[1], in3[1])
    gain_out[...] = gain[...] + gain_in[...]


def xl_body(t0, crossing, gain, gain_in, ours, others, gain_out):
    ours[...] = add_low(t0[0], crossing[0])
    others[...] = add_low(t0[1], crossing[1])
    gain_out[...] = gain[...] + gain_in[...]


def core_body(half_ref, ours, theirs, s0, s1, s2, s3):
    @pl.when(half_ref[0] == 0)
    def _():
        s0[...], s1[...], s2[...], s3[...] = ours[0], ours[1], theirs[0], theirs[1]

    @pl.when(half_ref[0] != 0)
    def _():
        s0[...], s1[...], s2[...], s3[...] = theirs[0], theirs[1], ours[0], ours[1]


def gain_body(gain, gain_in, gain_out):
    gain_out[...] = gain[...] + gain_in[...]


def zh_body(kept, b1, b2, b3, gain, gain_in, unit, gain_out):
    unit[...] = add_low(kept[...], b1[...], b2[...], b3[...])
    gain_out[...] = gain[...] + gain_in[...]


def rows_gain_body(u0, u1, u2, u3, gain, gain_in, rows, gain_out):
    rows[0], rows[1], rows[2], rows[3] = u0[...], u1[...], u2[...], u3[...]
    gain_out[...] = gain[...] + gain_in[...]


def shift(x, axes, by):
    count = lax.axis_size(axes)
    return lax.ppermute(x, axes, [(i, (i + by) % count) for i in range(count)])


def swap(x, axes, mask):
    count = lax.axis_size(axes)
    return lax.ppermute(x, axes, [(i, i ^ mask) for i in range(count)])


def shift_both(x, by):
    rows, cols = lax.axis_size(ROW), lax.axis_size(LON)
    pairs = [
        (r * cols + c, (r + by) % rows * cols + (c + by) % cols)
        for r in range(rows)
        for c in range(cols)
    ]
    return lax.ppermute(x, ALL, pairs)


def quarters(*arrays):
    arrays = [x.transpose(0, 2, 1, 3) for x in arrays]
    lon = WLON // 2

    def cut(rows, cols):
        return jnp.stack([x[rows, cols].reshape(QUARTER, D) for x in arrays])

    first, last = slice(0, CLAT), slice(CLAT, 2 * CLAT)
    west, east = slice(0, lon), slice(lon, WLON)
    below = shift(cut(first, east), ROW, -1)
    corner = shift_both(cut(first, west), -1)
    right = shift(cut(last, west), LON, -1)
    return cut(last, east), right, below, corner


def back_home(before, own, right, below, corner):
    below, corner, right = shift(below, ROW, 1), shift_both(corner, 1), shift(right, LON, 1)
    below, corner, right, _ = lax.optimization_barrier((below, corner, right, before))
    own, right, below, corner = (
        x.reshape(2, CLAT, WLON // 2, LEV, D) for x in (own, right, below, corner)
    )
    top = jnp.concatenate([corner, below], axis=2)
    bottom = jnp.concatenate([right, own], axis=2)
    both = jnp.concatenate([top, bottom], axis=1).transpose(0, 1, 3, 2, 4)
    return both[0], both[1]


def weight_unit(w_qkv, w_out, place):
    qkv = lax.dynamic_slice(w_qkv.transpose(1, 0, 2), (0, place * BLK, 0), (3, BLK, BLK))
    out = lax.dynamic_slice(w_out, (0, place * BLK), (BLK, BLK)).T
    return jnp.concatenate([qkv, out[None]], axis=0)


def shards(tokens, norm_gain, w_qkv, w_out, grad_out):
    zh, lat, xl, core = (lax.axis_index(a) for a in ("zh", "lat", "xl", "core"))
    half = ((zh // 2) ^ core).reshape(1)
    chips = {(s, t): (lat ^ s) * 2 + (xl ^ t) for s in range(4) for t in range(2)}
    pos = jnp.stack([chips[place] * 2 + (core ^ c) for place in sorted(chips) for c in range(2)])
    ends = jnp.stack(
        [lat ^ s for s in range(4)] + [(xl ^ t) * 2 + (core ^ c) for c in range(2) for t in range(2)]
    )
    edge = jnp.logical_and(zh == 3, lat == 3)
    owners = lax.axis_index(NEAR) ^ (jnp.arange(SLOTS) % 4)
    cut = jnp.logical_and(edge, owners == 3).astype(jnp.int32)
    gain_row = norm_gain.reshape(1, D)
    token = shaped((8, BLK), f32)
    window, windows = shaped((WIN, D)), shaped((4 * WIN, D))
    scalar = {0: smem}

    unit = weight_unit(w_qkv, w_out, pos[0])
    units = [unit] + [swap(unit, "zh", s) for s in (1, 2, 3)]
    pieces = quarters(tokens, grad_out)
    keep, give = small(select_body, [half] + units, [shaped(PAIR)] * 2, specs=scalar, name="select")
    given = swap(give, "core", 1)
    buffer = [pltpu.VMEM((WIN, D), f32)]
    rolled, cotangent, normed = small(
        enter_body, [*pieces, gain_row], [window] * 3, before=[give], scratch=buffer, name="enter"
    )
    (mine,) = small(join_body, [keep, given], [shaped(FOUR)], before=[normed], name="join")
    near = swap(mine, "xl", 1)
    m1a, m3a = swap(mine, "lat", 1), swap(mine, "lat", 3)
    x1, x2 = swap(normed, NEAR, 1), swap(normed, NEAR, 2)
    (pin,) = small(pin_body, [], [token], before=[near, m1a, m3a], name="pin")
    m1b, m3b = swap(near, "lat", 1), swap(near, "lat", 3)
    o0 = swap(m1a, "lat", 3)
    (pin,) = small(pin_body, [], [token], before=[m1b, m3b, x1, x2, pin], name="pin")
    o1 = swap(m3b, "lat", 1)
    x3 = swap(lax.optimization_barrier((x1, pin))[0], NEAR, 2)
    (x_own,) = small(rows_body, [normed, x1, x2, x3], [windows], before=[o0, o1, pin], name="rows")
    x_sib = swap(x_own, "core", 1)
    c1, c2, c3 = (swap(cotangent, NEAR, s) for s in (1, 2, 3))

    weights = [mine, near, m1a, m1b, o0, o1, m3a, m3b]
    qkv, att, p, wq, wo = forward(cut, pos, x_own, x_sib, weights)
    (c_own,) = small(rows_body, [cotangent, c1, c2, c3], [windows], before=[wo], name="rows")
    c_sib = swap(c_own, "core", 1)
    b_own, b_sib = branch_product(att, wo, c_own)
    b_other = swap(b_sib, "core", 1)
    wq_in = swap(lax.optimization_barrier((wq, b_own))[0], "core", 1)
    dp, dp_sent = backward(c_own, c_sib, qkv, p, wo, b_own)
    dp_in = swap(dp_sent, "core", 1)
    xs, cots = (x_own, x_sib), (c_own, c_sib)

    far0, far1 = grads([chips[2, 0], chips[2, 1]], core, xs, cots, dp, att, dp)
    back3, back1 = swap(far0, "lat", 1), swap(far1, "lat", 3)
    near_chips = [chips[s, t] for s in (1, 3, 0) for t in range(2)]
    g10, g11, g30, g31, g00, g01 = grads(near_chips, core, xs, cots, dp, att, far0)
    to1, to3 = small(
        sides_body, [g10, g11, g30, g31, back1, back3], [shaped((2,) + FOUR)] * 2, name="sides"
    )
    in1, in3 = swap(to1, "lat", 1), swap(to3, "lat", 3)
    first, second = pl.BlockSpec((WIN, D), lambda i: (0, 0)), pl.BlockSpec((WIN, D), lambda i: (1, 0))
    pair = shaped((2 * WIN, D))
    b_lead, b_pair = small(windows_body, [b_own, b_other], [pair] * 2, before=[to1], name="windows")
    b_in = swap(b_pair, NEAR, 1)
    d_lead, d_pair, gain = rolled_gradient(dp, dp_in, wq, wq_in, x_own, b_pair)
    d_in = swap(d_pair, NEAR, 2)

    gain, gain_shape = gain.reshape(GAIN), shaped(GAIN, f32)
    gain_in = swap(gain, ALL, 1)
    t0, t1, gain = small(
        lat_body,
        [g00, g01, in1, in3, gain, gain_in],
        [shaped(FOUR), shaped(FOUR), gain_shape],
        name="lat_sum",
    )
    crossing, gain_in = swap(t1, "xl", 1), swap(gain, ALL, 4)
    b_mid, gain = small(
        gain_mid_body,
        [b_lead, b_in, gain, gain_in],
        [window, gain_shape],
        before=[t1],
        specs={0: second, 1: second},
        name="mid",
    )
    b_last, gain_in = swap(b_mid, NEAR, 2), swap(gain, ALL, 8)
    ours, others, gain = small(
        xl_body,
        [t0, crossing, gain, gain_in],
        [shaped(PAIR)] * 2 + [gain_shape],
        before=[b_mid],
        name="xl_sum",
    )
    theirs = swap(others, "core", 1)
    (d_mid,) = small(
        mid_body, [d_lead, d_in], [window], before=[ours], specs={0: second, 1: second}, name="mid"
    )
    d_last = swap(d_mid, NEAR, 1)
    sent = small(
        core_body,
        [half, ours, theirs],
        [shaped(UNIT)] * 4,
        before=[d_mid, b_last],
        specs=scalar,
        name="core_sum",
    )
    back = [swap(sent[s], "zh", s) for s in (1, 2, 3)]
    gain_in = swap(lax.optimization_barrier((gain, sent[0]))[0], ALL, 2)
    (gain,) = small(gain_body, [gain, gain_in], [gain_shape], before=[sent[1], d_last], name="gain")
    gain_in = swap(gain, ALL, 64)
    unit, gain = small(
        zh_body, [sent[0], *back, gain, gain_in], [shaped(UNIT), gain_shape], name="zh_sum"
    )
    around, gain_in = [swap(unit, "lat", s) for s in (1, 2, 3)], swap(gain, ALL, 128)
    results = small(
        leave_body,
        [rolled, cotangent, gain_row, b_lead, b_in, b_last, d_lead, d_in, d_last],
        [shaped((2, QUARTER, D))] * 4,
        before=[unit],
        specs={n: first for n in (3, 4, 6, 7)},
        scratch=buffer,
        name="leave",
    )
    rows, gain = small(
        rows_gain_body,
        [unit, *around, gain, gain_in],
        [shaped((4,) + UNIT), gain_shape],
        before=[results[0]],
        name="slices",
    )
    near_rows, core_rows = swap(rows, "xl", 1), swap(rows, "core", 1)
    results, _ = lax.optimization_barrier((results, rows))
    output, grad_tokens = back_home(rows, *results)
    near_rows, output, _ = lax.optimization_barrier((near_rows, output, grad_tokens))
    last_rows = swap(near_rows, "core", 1)
    grad_wqkv, grad_wout, gain = finish(
        ends, [rows, near_rows, core_rows, last_rows], gain, swap(gain, ALL, 16)
    )
    grad_gain = (gain + swap(gain, ALL, 32)).reshape(D) / norm_gain
    return output, grad_tokens, grad_wqkv.transpose(1, 0, 2), grad_wout, grad_gain


def solution(mesh):
    fine = Mesh(mesh.devices.reshape(4, 2, 2, 4, 2, 2), ALL)
    by_token = P(ROW, None, LON, None)
    in_specs = (by_token, P(), P(None, None, OUTER), P(OUTER, None), by_token)
    out_specs = (by_token, by_token, P(None, None, OUTER), P(OUTER, None), P())
    return jax.shard_map(shards, mesh=fine, in_specs=in_specs, out_specs=out_specs, check_vma=False)
```

```python
import functools

import jax
import jax.numpy as jnp
from jax import lax
from jax.experimental import pallas as pl
from jax.experimental.pallas import tpu as pltpu
from jax.sharding import Mesh, PartitionSpec as P

D = 2048
HEAD = 64
LEV = 2
CLAT = 3
WLON = 12
WIN = 2 * CLAT * LEV * WLON
HALF = WIN // 2
SLOTS = 8
STEP = 2
ROWS = STEP * WIN
TOK = SLOTS * WIN
COLS = 256
HEADS_DEV = COLS // HEAD
SCALE = HEAD ** (-0.5)
BLK = 128
EPSILON = 1e-05
bf16 = jnp.bfloat16
f32 = jnp.float32

ALL = ("zh", "zl", "xh", "lat", "xl", "core")
OUTER = ("zh", "zl", "xh")
ROW = ("zh", "zl", "xh", "lat")
LON = ("xl", "core")
NEAR = ("zl", "xh")


def nn(a, b):
    return lax.dot_general(a, b, (((1,), (0,)), ((), ())), preferred_element_type=f32)


def nt(a, b):
    return lax.dot_general(a, b, (((1,), (1,)), ((), ())), preferred_element_type=f32)


def tn(a, b):
    return lax.dot_general(a, b, (((0,), (0,)), ((), ())), preferred_element_type=f32)


def assemble(pos_ref, pieces, wq_ref, wo_ref):
    for n, piece in enumerate(pieces):
        for c in range(2):
            rows = pl.ds(pl.multiple_of(pos_ref[2 * n + c] * BLK, BLK), BLK)
            for blk in range(2):
                for i in range(3):
                    wq_ref[rows, (2 * i + blk) * BLK : (2 * i + blk + 1) * BLK] = piece[c, blk, i]
                wo_ref[rows, blk * BLK : (blk + 1) * BLK] = piece[c, blk, 3]


def choose(step, own_ref, sib_ref, out_ref):
    @pl.when(step < HALF_STEPS)
    def _():
        out_ref[...] = own_ref[...]

    @pl.when(step >= HALF_STEPS)
    def _():
        out_ref[...] = sib_ref[...]


def forward_kernel(cut_ref, pos_ref, own_ref, sib_ref, *refs):
    pieces, (qkv_ref, att_ref, p_ref, wq_ref, wo_ref, x_ref) = refs[:8], refs[8:]
    step = pl.program_id(0)

    @pl.when(step == 0)
    def _():
        assemble(pos_ref, pieces, wq_ref, wo_ref)

    choose(step, own_ref, sib_ref, x_ref)
    for n in range(3):
        cols = slice(n * COLS, (n + 1) * COLS)
        qkv_ref[:, cols] = nn(x_ref[...], wq_ref[:, cols]).astype(bf16)
    row = lax.broadcasted_iota(jnp.int32, (WIN, WIN), 0) >= HALF
    col = lax.broadcasted_iota(jnp.int32, (WIN, WIN), 1) >= HALF
    same = row == col
    for w in range(STEP):
        rows = slice(w * WIN, (w + 1) * WIN)
        allowed = jnp.logical_or(same, cut_ref[step * STEP + w] == 0)
        for h in range(HEADS_DEV):
            q = qkv_ref[rows, h * HEAD : (h + 1) * HEAD]
            k = qkv_ref[rows, COLS + h * HEAD : COLS + (h + 1) * HEAD]
            v = qkv_ref[rows, 2 * COLS + h * HEAD : 2 * COLS + (h + 1) * HEAD]
            s = jnp.where(allowed, nt(q * bf16(SCALE), k), -1e30)
            e = jnp.exp(s - jnp.max(s, -1, keepdims=True))
            p = e * (1.0 / jnp.sum(e, -1, keepdims=True))
            p_ref[w, h] = p
            att_ref[rows, h * HEAD : (h + 1) * HEAD] = nn(p.astype(bf16), v).astype(bf16)


def backward_kernel(own_ref, sib_ref, qkv_ref, p_ref, wo_ref, _, dp_ref, sent_ref, cot_ref):
    choose(pl.program_id(0), own_ref, sib_ref, cot_ref)
    d_att = nn(cot_ref[...], wo_ref[...]).astype(bf16)
    for w in range(STEP):
        rows = slice(w * WIN, (w + 1) * WIN)
        for h in range(HEADS_DEV):
            q = qkv_ref[rows, h * HEAD : (h + 1) * HEAD]
            k = qkv_ref[rows, COLS + h * HEAD : COLS + (h + 1) * HEAD]
            v = qkv_ref[rows, 2 * COLS + h * HEAD : 2 * COLS + (h + 1) * HEAD]
            p = p_ref[w, h]
            d_o = d_att[rows, h * HEAD : (h + 1) * HEAD]
            d_w = nt(d_o, v)
            dots = jnp.sum(p * d_w, -1, keepdims=True)
            d_s = (p * (d_w - dots) * SCALE).astype(bf16)
            dp_ref[rows, h * HEAD : (h + 1) * HEAD] = nn(d_s, k).astype(bf16)
            dp_ref[rows, COLS + h * HEAD : COLS + (h + 1) * HEAD] = tn(d_s, q).astype(bf16)
            dp_ref[rows, 2 * COLS + h * HEAD : 2 * COLS + (h + 1) * HEAD] = tn(p.astype(bf16), d_o).astype(bf16)

    @pl.when(pl.program_id(0) >= HALF_STEPS)
    def _():
        sent_ref[...] = dp_ref[...]


def grads_kernel(count, where_ref, xa_ref, xb_ref, ca_ref, cb_ref, dp_ref, att_ref, _, *refs):
    step = pl.program_id(0)
    core = where_ref[count]
    g_refs, (x_ref, cot_ref) = refs[:count], refs[count:]
    x_ref[:PART, :], x_ref[PART:, :] = xa_ref[...], xb_ref[...]
    cot_ref[:PART, :], cot_ref[PART:, :] = ca_ref[...], cb_ref[...]
    gq = tn(x_ref[...], dp_ref[...]).astype(bf16)
    go = tn(cot_ref[...], att_ref[...]).astype(bf16)
    for n, g_ref in enumerate(g_refs):

        @pl.when(step == n)
        def _():
            for part in range(2):
                rows = slice(part * BLK, (part + 1) * BLK)
                place = part ^ core
                for blk in range(2):
                    for i in range(3):
                        g_ref[place, blk, i] = gq[rows, (2 * i + blk) * BLK : (2 * i + blk + 1) * BLK]
                    g_ref[place, blk, 3] = go[rows, blk * BLK : (blk + 1) * BLK]


def product(lead, out, pair, slots):
    for n, (ref, at) in enumerate(slots):
        target = pair if ref else lead
        target[at * WIN : (at + 1) * WIN, :] = out[n * WIN : (n + 1) * WIN, :]


def rolled_kernel(dp_ref, in_ref, w_ref, other_ref, x_ref, _, lead_ref, pair_ref, gain_ref):
    total = nt(dp_ref[...], w_ref[...]) + nt(in_ref[...], other_ref[...])
    product(lead_ref, total.astype(bf16), pair_ref, ((0, 0), (0, 1), (1, 0), (1, 1)))
    gain_ref[...] = jnp.sum(total * x_ref[...].astype(f32), 0, keepdims=True)


def branch_kernel(att_ref, w_ref, _, own_ref, sib_ref):
    total = nt(att_ref[...], w_ref[...]).astype(bf16)
    own_ref[...] = total[:PART]
    sib_ref[...] = total[PART:]


def finish_kernel(where_ref, a_ref, b_ref, c_ref, d_ref, gq_ref, go_ref):
    for n, ref in enumerate((a_ref, b_ref, c_ref, d_ref)):
        rows = pl.ds(pl.multiple_of(where_ref[4 + n] * BLK, BLK), BLK)
        for i in range(3):
            gq_ref[i, rows, :] = ref[0, i].astype(f32)
        go_ref[:, rows] = ref[0, 3].astype(f32).T


def params():
    return pltpu.CompilerParams(dimension_semantics=("arbitrary",), vmem_limit_bytes=63 * 1024 * 1024)


PART = TOK // 2
HALF_STEPS = SLOTS // STEP // 2
own_spec = pl.BlockSpec((ROWS, D), lambda i: (jnp.minimum(i, HALF_STEPS - 1), 0))
sib_spec = pl.BlockSpec((ROWS, D), lambda i: (jnp.maximum(i - HALF_STEPS, 0), 0))
p_spec = pl.BlockSpec((STEP, HEADS_DEV, WIN, WIN), lambda i: (i, 0, 0, 0))
smem = pl.BlockSpec(memory_space=pltpu.SMEM)
unread = pl.BlockSpec(memory_space=pl.ANY)
WIDE, STRIP = 1024, 512
strip_column = pl.BlockSpec((PART, STRIP), lambda i: (0, i))
wide_column = pl.BlockSpec((PART, WIDE), lambda i: (0, i))


def rows_spec(cols):
    return pl.BlockSpec((ROWS, cols), lambda i: (i, 0))


def later_spec(cols):
    return pl.BlockSpec((ROWS, cols), lambda i: (jnp.maximum(i - HALF_STEPS, 0), 0))


def whole(*shape):
    return pl.BlockSpec(shape, lambda *i: (0,) * len(shape))


def shaped(shape, dtype=bf16):
    return jax.ShapeDtypeStruct(shape, dtype)


def forward(cut, pos, own, sib, weights):
    return pl.pallas_call(
        forward_kernel,
        grid=(SLOTS // STEP,),
        in_specs=[smem, smem, own_spec, sib_spec] + [whole(*w.shape) for w in weights],
        out_specs=[
            rows_spec(3 * COLS),
            rows_spec(COLS),
            p_spec,
            whole(D, 3 * COLS),
            whole(D, COLS),
        ],
        out_shape=[
            shaped((TOK, 3 * COLS)),
            shaped((TOK, COLS)),
            shaped((SLOTS, HEADS_DEV, WIN, WIN), f32),
            shaped((D, 3 * COLS)),
            shaped((D, COLS)),
        ],
        scratch_shapes=[pltpu.VMEM((ROWS, D), bf16)],
        compiler_params=params(),
        name="attention_forward",
    )(cut, pos, own, sib, *weights)


def backward(own, sib, qkv, p, wo, before):
    return pl.pallas_call(
        backward_kernel,
        grid=(SLOTS // STEP,),
        in_specs=[own_spec, sib_spec, rows_spec(3 * COLS), p_spec, whole(D, COLS), unread],
        out_specs=[rows_spec(3 * COLS), later_spec(3 * COLS)],
        out_shape=[shaped((TOK, 3 * COLS)), shaped((PART, 3 * COLS))],
        scratch_shapes=[pltpu.VMEM((ROWS, D), bf16)],
        compiler_params=params(),
        name="attention_backward",
    )(own, sib, qkv, p, wo, before)


def grads(chips, core, xs, cots, dp, att, before):
    count = len(chips)
    part = pl.BlockSpec((PART, 2 * BLK), lambda i, where: (0, where[i]))
    return pl.pallas_call(
        functools.partial(grads_kernel, count),
        grid_spec=pltpu.PrefetchScalarGridSpec(
            num_scalar_prefetch=1,
            grid=(count,),
            in_specs=[part] * 4 + [whole(TOK, 3 * COLS), whole(TOK, COLS), unread],
            out_specs=[whole(2, 2, 4, BLK, BLK)] * count,
            scratch_shapes=[pltpu.VMEM((TOK, 2 * BLK), bf16)] * 2,
        ),
        out_shape=[shaped((2, 2, 4, BLK, BLK))] * count,
        compiler_params=params(),
        name="weight_gradients",
    )(jnp.stack(list(chips) + [core]), *xs, *cots, dp, att, before)


def rolled_gradient(dp, dp_in, wq, wq_in, x, before):
    depth = 3 * COLS
    strip = pl.BlockSpec((STRIP, depth), lambda i: (i, 0))
    half = pl.BlockSpec((PART // 2, STRIP), lambda i: (0, i))
    return pl.pallas_call(
        rolled_kernel,
        grid=(D // STRIP,),
        in_specs=[whole(PART, depth)] * 2 + [strip] * 2 + [strip_column, unread],
        out_specs=[half, half, pl.BlockSpec((1, STRIP), lambda i: (0, i))],
        out_shape=[shaped((PART // 2, D))] * 2 + [shaped((1, D), f32)],
        compiler_params=params(),
        name="rolled_gradient",
    )(dp, dp_in, wq, wq_in, x, before)


def branch_product(att, wo, before):
    return pl.pallas_call(
        branch_kernel,
        grid=(D // WIDE,),
        in_specs=[whole(TOK, COLS), pl.BlockSpec((WIDE, COLS), lambda i: (i, 0)), unread],
        out_specs=[wide_column, wide_column],
        out_shape=[shaped((PART, D))] * 2,
        compiler_params=params(),
        name="branch_product",
    )(att, wo, before)


def finish(where, parts):
    return pl.pallas_call(
        finish_kernel,
        grid_spec=pltpu.PrefetchScalarGridSpec(
            num_scalar_prefetch=1,
            grid=(4,),
            in_specs=[pl.BlockSpec((1, 4, BLK, BLK), lambda s, where: (s, 0, 0, 0))] * 4,
            out_specs=[
                pl.BlockSpec((3, 4 * BLK, BLK), lambda s, where: (0, where[s], 0)),
                pl.BlockSpec((BLK, 4 * BLK), lambda s, where: (0, where[s])),
            ],
        ),
        out_shape=[shaped((3, D, BLK), f32), shaped((BLK, D), f32)],
        compiler_params=params(),
        name="finish_gradients",
    )(where, *parts)


def small(body, ins, outs, before=(), specs=(), scratch=(), name=None):
    specs = dict(specs)
    in_specs = [specs.get(n, whole(*x.shape)) for n, x in enumerate(ins)] + [unread] * len(before)
    count, extra = len(ins), len(before)

    def kernel(*refs):
        body(*refs[:count], *refs[count + extra :])

    return pl.pallas_call(
        kernel,
        grid=(1,),
        in_specs=in_specs,
        out_specs=[whole(*x.shape) for x in outs],
        out_shape=list(outs),
        scratch_shapes=list(scratch),
        compiler_params=params(),
        name=name,
    )(*ins, *before)


QUARTER = WIN // 4
UNIT = (4, BLK, BLK)
PAIR = (2,) + UNIT
FOUR = (2, 2) + UNIT
GAIN = (16, BLK)


def wide(*refs):
    total = refs[0].astype(f32)
    for ref in refs[1:]:
        total = total + ref.astype(f32)
    return total


def add_low(*values):
    return wide(*values).astype(bf16)


def select_body(half_ref, u0, u1, u2, u3, keep, give):
    @pl.when(half_ref[0] == 0)
    def _():
        keep[0], keep[1], give[0], give[1] = u0[...], u1[...], u2[...], u3[...]

    @pl.when(half_ref[0] != 0)
    def _():
        keep[0], keep[1], give[0], give[1] = u2[...], u3[...], u0[...], u1[...]


def join_body(*refs):
    out = refs[-1]
    for n, ref in enumerate(refs[:-1]):
        out[n] = ref[...]


def rows_body(*refs):
    out = refs[-1]
    for n, ref in enumerate(refs[:-1]):
        out[n * WIN : (n + 1) * WIN, :] = ref[...]


def pin_body(out):
    out[...] = jnp.zeros_like(out)


def normal(values):
    centered = values - jnp.mean(values, -1, keepdims=True)
    inverse_std = lax.rsqrt(jnp.mean(centered * centered, -1, keepdims=True) + EPSILON)
    return centered * inverse_std, inverse_std


def enter_body(own, right, below, corner, gain, rolled, cot, normed, buffer):
    for n, out in enumerate((rolled, cot)):
        for k, piece in enumerate((own, right, below, corner)):
            buffer[k * QUARTER : (k + 1) * QUARTER, :] = piece[n].astype(f32)
        out[...] = buffer[...].astype(bf16)
        if n == 0:
            normed[...] = (normal(buffer[...])[0] * gain[...]).astype(bf16)


def leave_body(rolled, cot, gain, b0, b1, b2, d0, d1, d2, own, right, below, corner, buffer):
    branch = add_low(b0[...], b1[...], b2[...])
    buffer[...] = rolled[...].astype(f32) + branch.astype(f32)
    for k, piece in enumerate((own, right, below, corner)):
        piece[0] = buffer[k * QUARTER : (k + 1) * QUARTER, :].astype(bf16)
    standard, inverse_std = normal(rolled[...].astype(f32))
    scaled = add_low(d0[...], d1[...], d2[...]).astype(f32) * gain[...]
    local = inverse_std * (
        scaled
        - jnp.mean(scaled, -1, keepdims=True)
        - standard * jnp.mean(scaled * standard, -1, keepdims=True)
    )
    buffer[...] = cot[...].astype(f32) + local
    for k, piece in enumerate((own, right, below, corner)):
        piece[1] = buffer[k * QUARTER : (k + 1) * QUARTER, :].astype(bf16)


def windows_body(own, other, lead, pair):
    for n, (out, at) in enumerate(((lead, 0), (pair, 0), (lead, 1), (pair, 1))):
        rows = slice(n * WIN, (n + 1) * WIN)
        out[at * WIN : (at + 1) * WIN, :] = add_low(own[rows, :], other[rows, :])


def mid_body(lead, given, out):
    out[...] = add_low(lead[...], given[...])


def gain_mid_body(lead, given, gain, gain_in, out, gain_out):
    mid_body(lead, given, out)
    gain_out[...] = gain[...] + gain_in[...]


def sides_body(g10, g11, g30, g31, back1, back3, to1, to3):
    to1[0], to1[1] = g10[...], add_low(g11[...], back1[...])
    to3[0], to3[1] = add_low(g30[...], back3[...]), g31[...]


def lat_body(g00, g01, in1, in3, gain, gain_in, t0, t1, gain_out):
    t0[...] = add_low(g00[...], in1[0], in3[0])
    t1[...] = add_low(g01[...], in1[1], in3[1])
    gain_out[...] = gain[...] + gain_in[...]


def xl_body(t0, crossing, gain, gain_in, ours, others, gain_out):
    ours[...] = add_low(t0[0], crossing[0])
    others[...] = add_low(t0[1], crossing[1])
    gain_out[...] = gain[...] + gain_in[...]


def core_body(half_ref, ours, theirs, gain, gain_in, s0, s1, s2, s3, gain_out):
    gain_out[...] = gain[...] + gain_in[...]

    @pl.when(half_ref[0] == 0)
    def _():
        s0[...], s1[...], s2[...], s3[...] = ours[0], ours[1], theirs[0], theirs[1]

    @pl.when(half_ref[0] != 0)
    def _():
        s0[...], s1[...], s2[...], s3[...] = theirs[0], theirs[1], ours[0], ours[1]


def gain_body(gain, gain_in, gain_out):
    gain_out[...] = gain[...] + gain_in[...]


def zh_body(kept, b1, b2, b3, gain, gain_in, unit, gain_out):
    unit[...] = add_low(kept[...], b1[...], b2[...], b3[...])
    gain_out[...] = gain[...] + gain_in[...]


def rows_gain_body(u0, u1, u2, u3, gain, gain_in, rows, gain_out):
    rows[0], rows[1], rows[2], rows[3] = u0[...], u1[...], u2[...], u3[...]
    gain_out[...] = gain[...] + gain_in[...]


def shift(x, axes, by):
    count = lax.axis_size(axes)
    return lax.ppermute(x, axes, [(i, (i + by) % count) for i in range(count)])


def swap(x, axes, mask):
    count = lax.axis_size(axes)
    return lax.ppermute(x, axes, [(i, i ^ mask) for i in range(count)])


def shift_both(x, by):
    rows, cols = lax.axis_size(ROW), lax.axis_size(LON)
    pairs = [
        (r * cols + c, (r + by) % rows * cols + (c + by) % cols)
        for r in range(rows)
        for c in range(cols)
    ]
    return lax.ppermute(x, ALL, pairs)


def quarters(*arrays):
    arrays = [x.transpose(0, 2, 1, 3) for x in arrays]
    lon = WLON // 2

    def cut(rows, cols):
        return jnp.stack([x[rows, cols].reshape(QUARTER, D) for x in arrays])

    first, last = slice(0, CLAT), slice(CLAT, 2 * CLAT)
    west, east = slice(0, lon), slice(lon, WLON)
    below = shift(cut(first, east), ROW, -1)
    corner = shift_both(cut(first, west), -1)
    right = shift(cut(last, west), LON, -1)
    return cut(last, east), right, below, corner


def back_home(before, own, right, below, corner):
    below, corner, right = shift(below, ROW, 1), shift_both(corner, 1), shift(right, LON, 1)
    below, corner, right, _ = lax.optimization_barrier((below, corner, right, before))
    own, right, below, corner = (
        x.reshape(2, CLAT, WLON // 2, LEV, D) for x in (own, right, below, corner)
    )
    top = jnp.concatenate([corner, below], axis=2)
    bottom = jnp.concatenate([right, own], axis=2)
    both = jnp.concatenate([top, bottom], axis=1).transpose(0, 1, 3, 2, 4)
    return both[0], both[1]


def weight_unit(w_qkv, w_out, place):
    qkv = lax.dynamic_slice(w_qkv.transpose(1, 0, 2), (0, place * BLK, 0), (3, BLK, BLK))
    out = lax.dynamic_slice(w_out, (0, place * BLK), (BLK, BLK)).T
    return jnp.concatenate([qkv, out[None]], axis=0)


def shards(tokens, norm_gain, w_qkv, w_out, grad_out):
    zh, lat, xl, core = (lax.axis_index(a) for a in ("zh", "lat", "xl", "core"))
    half = ((zh // 2) ^ core).reshape(1)
    chips = {(s, t): (lat ^ s) * 2 + (xl ^ t) for s in range(4) for t in range(2)}
    pos = jnp.stack([chips[place] * 2 + (core ^ c) for place in sorted(chips) for c in range(2)])
    ends = jnp.stack(
        [lat ^ s for s in range(4)] + [(xl ^ t) * 2 + (core ^ c) for c in range(2) for t in range(2)]
    )
    edge = jnp.logical_and(zh == 3, lat == 3)
    owners = lax.axis_index(NEAR) ^ (jnp.arange(SLOTS) % 4)
    cut = jnp.logical_and(edge, owners == 3).astype(jnp.int32)
    gain_row = norm_gain.reshape(1, D)
    token = shaped((8, BLK), f32)
    window, windows = shaped((WIN, D)), shaped((4 * WIN, D))
    scalar = {0: smem}

    unit = weight_unit(w_qkv, w_out, pos[0])
    units = [unit] + [swap(unit, "zh", s) for s in (1, 2, 3)]
    pieces = quarters(tokens, grad_out)
    keep, give = small(select_body, [half] + units, [shaped(PAIR)] * 2, specs=scalar, name="select")
    given = swap(give, "core", 1)
    buffer = [pltpu.VMEM((WIN, D), f32)]
    rolled, cotangent, normed = small(
        enter_body, [*pieces, gain_row], [window] * 3, before=[give], scratch=buffer, name="enter"
    )
    (mine,) = small(join_body, [keep, given], [shaped(FOUR)], before=[normed], name="join")
    near = swap(mine, "xl", 1)
    m1a, m3a = swap(mine, "lat", 1), swap(mine, "lat", 3)
    x1, x2 = swap(normed, NEAR, 1), swap(normed, NEAR, 2)
    (pin,) = small(pin_body, [], [token], before=[near, m1a, m3a], name="pin")
    m1b, m3b = swap(near, "lat", 1), swap(near, "lat", 3)
    o0 = swap(m1a, "lat", 3)
    (pin,) = small(pin_body, [], [token], before=[m1b, m3b, x1, x2, pin], name="pin")
    o1 = swap(m3b, "lat", 1)
    x3 = swap(lax.optimization_barrier((x1, pin))[0], NEAR, 2)
    (x_own,) = small(rows_body, [normed, x1, x2, x3], [windows], before=[o0, o1, pin], name="rows")
    x_sib = swap(x_own, "core", 1)
    c1, c2, c3 = (swap(cotangent, NEAR, s) for s in (1, 2, 3))

    weights = [mine, near, m1a, m1b, o0, o1, m3a, m3b]
    qkv, att, p, wq, wo = forward(cut, pos, x_own, x_sib, weights)
    (c_own,) = small(rows_body, [cotangent, c1, c2, c3], [windows], before=[wo], name="rows")
    c_sib = swap(c_own, "core", 1)
    b_own, b_sib = branch_product(att, wo, c_own)
    b_other = swap(b_sib, "core", 1)
    wq_in = swap(lax.optimization_barrier((wq, b_own))[0], "core", 1)
    dp, dp_sent = backward(c_own, c_sib, qkv, p, wo, b_own)
    dp_in = swap(dp_sent, "core", 1)
    xs, cots = (x_own, x_sib), (c_own, c_sib)

    far0, far1 = grads([chips[2, 0], chips[2, 1]], core, xs, cots, dp, att, dp)
    back3, back1 = swap(far0, "lat", 1), swap(far1, "lat", 3)
    near_chips = [chips[s, t] for s in (1, 3, 0) for t in range(2)]
    g10, g11, g30, g31, g00, g01 = grads(near_chips, core, xs, cots, dp, att, far0)
    to1, to3 = small(
        sides_body, [g10, g11, g30, g31, back1, back3], [shaped((2,) + FOUR)] * 2, name="sides"
    )
    in1, in3 = swap(to1, "lat", 1), swap(to3, "lat", 3)
    first, second = pl.BlockSpec((WIN, D), lambda i: (0, 0)), pl.BlockSpec((WIN, D), lambda i: (1, 0))
    pair = shaped((2 * WIN, D))
    b_lead, b_pair = small(windows_body, [b_own, b_other], [pair] * 2, before=[to1], name="windows")
    b_in = swap(b_pair, NEAR, 1)
    d_lead, d_pair, gain = rolled_gradient(dp, dp_in, wq, wq_in, x_own, b_pair)
    d_in = swap(d_pair, NEAR, 2)

    gain, gain_shape = gain.reshape(GAIN), shaped(GAIN, f32)
    gain_in = swap(gain, ALL, 1)
    (gain,) = small(gain_body, [gain, gain_in], [gain_shape], before=[d_pair], name="gain")
    gain_in = swap(gain, ALL, 4)
    t0, t1, gain = small(
        lat_body,
        [g00, g01, in1, in3, gain, gain_in],
        [shaped(FOUR), shaped(FOUR), gain_shape],
        name="lat_sum",
    )
    crossing, gain_in = swap(t1, "xl", 1), swap(gain, ALL, 8)
    b_mid, gain = small(
        gain_mid_body,
        [b_lead, b_in, gain, gain_in],
        [window, gain_shape],
        before=[t1],
        specs={0: second, 1: second},
        name="mid",
    )
    b_last, gain_in = swap(b_mid, NEAR, 2), swap(gain, ALL, 2)
    ours, others, gain = small(
        xl_body,
        [t0, crossing, gain, gain_in],
        [shaped(PAIR)] * 2 + [gain_shape],
        before=[b_mid],
        name="xl_sum",
    )
    theirs, gain_in = swap(others, "core", 1), swap(gain, ALL, 32)
    (d_mid,) = small(
        mid_body, [d_lead, d_in], [window], before=[ours], specs={0: second, 1: second}, name="mid"
    )
    d_last = swap(d_mid, NEAR, 1)
    *sent, gain = small(
        core_body,
        [half, ours, theirs, gain, gain_in],
        [shaped(UNIT)] * 4 + [gain_shape],
        before=[d_mid, b_last],
        specs=scalar,
        name="core_sum",
    )
    back = [swap(sent[s], "zh", s) for s in (1, 2, 3)]
    gain_in = swap(gain, ALL, 16)
    (gain,) = small(gain_body, [gain, gain_in], [gain_shape], before=[sent[1], d_last], name="gain")
    gain_in = swap(gain, ALL, 64)
    unit, gain = small(
        zh_body, [sent[0], *back, gain, gain_in], [shaped(UNIT), gain_shape], name="zh_sum"
    )
    around, gain_in = [swap(unit, "lat", s) for s in (1, 2, 3)], swap(gain, ALL, 128)
    results = small(
        leave_body,
        [rolled, cotangent, gain_row, b_lead, b_in, b_last, d_lead, d_in, d_last],
        [shaped((2, QUARTER, D))] * 4,
        before=[unit],
        specs={n: first for n in (3, 4, 6, 7)},
        scratch=buffer,
        name="leave",
    )
    rows, gain = small(
        rows_gain_body,
        [unit, *around, gain, gain_in],
        [shaped((4,) + UNIT), gain_shape],
        before=[results[0]],
        name="slices",
    )
    near_rows, core_rows = swap(rows, "xl", 1), swap(rows, "core", 1)
    results, _ = lax.optimization_barrier((results, rows))
    output, grad_tokens = back_home(rows, *results)
    near_rows, output, _ = lax.optimization_barrier((near_rows, output, grad_tokens))
    last_rows = swap(near_rows, "core", 1)
    grad_wqkv, grad_wout = finish(ends, [rows, near_rows, core_rows, last_rows])
    grad_gain = gain.reshape(D) / norm_gain
    return output, grad_tokens, grad_wqkv.transpose(1, 0, 2), grad_wout, grad_gain


def solution(mesh):
    fine = Mesh(mesh.devices.reshape(4, 2, 2, 4, 2, 2), ALL)
    by_token = P(ROW, None, LON, None)
    in_specs = (by_token, P(), P(None, None, OUTER), P(OUTER, None), by_token)
    out_specs = (by_token, by_token, P(None, None, OUTER), P(OUTER, None), P())
    return jax.shard_map(shards, mesh=fine, in_specs=in_specs, out_specs=out_specs, check_vma=False)
```

```python
import functools

import jax
import jax.numpy as jnp
from jax import lax
from jax.experimental import pallas as pl
from jax.experimental.pallas import tpu as pltpu
from jax.sharding import Mesh, PartitionSpec as P

D = 2048
HEAD = 64
LEV = 2
CLAT = 3
WLON = 12
WIN = 2 * CLAT * LEV * WLON
HALF = WIN // 2
SLOTS = 8
STEP = 2
ROWS = STEP * WIN
TOK = SLOTS * WIN
COLS = 256
HEADS_DEV = COLS // HEAD
SCALE = HEAD ** (-0.5)
BLK = 128
EPSILON = 1e-05
bf16 = jnp.bfloat16
f32 = jnp.float32

ALL = ("zh", "zl", "xh", "lat", "xl", "core")
OUTER = ("zh", "zl", "xh")
ROW = ("zh", "zl", "xh", "lat")
LON = ("xl", "core")
NEAR = ("zl", "xh")


def nn(a, b):
    return lax.dot_general(a, b, (((1,), (0,)), ((), ())), preferred_element_type=f32)


def nt(a, b):
    return lax.dot_general(a, b, (((1,), (1,)), ((), ())), preferred_element_type=f32)


def tn(a, b):
    return lax.dot_general(a, b, (((0,), (0,)), ((), ())), preferred_element_type=f32)


def assemble(pos_ref, pieces, wq_ref, wo_ref):
    for n, piece in enumerate(pieces):
        for c in range(2):
            rows = pl.ds(pl.multiple_of(pos_ref[2 * n + c] * BLK, BLK), BLK)
            for blk in range(2):
                for i in range(3):
                    wq_ref[rows, (2 * i + blk) * BLK : (2 * i + blk + 1) * BLK] = piece[c, blk, i]
                wo_ref[rows, blk * BLK : (blk + 1) * BLK] = piece[c, blk, 3]


def choose(step, own_ref, sib_ref, out_ref):
    @pl.when(step < HALF_STEPS)
    def _():
        out_ref[...] = own_ref[...]

    @pl.when(step >= HALF_STEPS)
    def _():
        out_ref[...] = sib_ref[...]


def forward_kernel(cut_ref, pos_ref, own_ref, sib_ref, *refs):
    pieces, (qkv_ref, att_ref, p_ref, wq_ref, wo_ref, x_ref) = refs[:8], refs[8:]
    step = pl.program_id(0)

    @pl.when(step == 0)
    def _():
        assemble(pos_ref, pieces, wq_ref, wo_ref)

    choose(step, own_ref, sib_ref, x_ref)
    for n in range(3):
        cols = slice(n * COLS, (n + 1) * COLS)
        qkv_ref[:, cols] = nn(x_ref[...], wq_ref[:, cols]).astype(bf16)
    row = lax.broadcasted_iota(jnp.int32, (WIN, WIN), 0) >= HALF
    col = lax.broadcasted_iota(jnp.int32, (WIN, WIN), 1) >= HALF
    same = row == col
    for w in range(STEP):
        rows = slice(w * WIN, (w + 1) * WIN)
        allowed = jnp.logical_or(same, cut_ref[step * STEP + w] == 0)
        for h in range(HEADS_DEV):
            q = qkv_ref[rows, h * HEAD : (h + 1) * HEAD]
            k = qkv_ref[rows, COLS + h * HEAD : COLS + (h + 1) * HEAD]
            v = qkv_ref[rows, 2 * COLS + h * HEAD : 2 * COLS + (h + 1) * HEAD]
            s = jnp.where(allowed, nt(q * bf16(SCALE), k), -1e30)
            e = jnp.exp(s - jnp.max(s, -1, keepdims=True))
            p = e * (1.0 / jnp.sum(e, -1, keepdims=True))
            p_ref[w, h] = p
            att_ref[rows, h * HEAD : (h + 1) * HEAD] = nn(p.astype(bf16), v).astype(bf16)


def backward_kernel(own_ref, sib_ref, qkv_ref, p_ref, wo_ref, _, dp_ref, sent_ref, cot_ref):
    choose(pl.program_id(0), own_ref, sib_ref, cot_ref)
    d_att = nn(cot_ref[...], wo_ref[...]).astype(bf16)
    for w in range(STEP):
        rows = slice(w * WIN, (w + 1) * WIN)
        for h in range(HEADS_DEV):
            q = qkv_ref[rows, h * HEAD : (h + 1) * HEAD]
            k = qkv_ref[rows, COLS + h * HEAD : COLS + (h + 1) * HEAD]
            v = qkv_ref[rows, 2 * COLS + h * HEAD : 2 * COLS + (h + 1) * HEAD]
            p = p_ref[w, h]
            d_o = d_att[rows, h * HEAD : (h + 1) * HEAD]
            d_w = nt(d_o, v)
            dots = jnp.sum(p * d_w, -1, keepdims=True)
            d_s = (p * (d_w - dots) * SCALE).astype(bf16)
            dp_ref[rows, h * HEAD : (h + 1) * HEAD] = nn(d_s, k).astype(bf16)
            dp_ref[rows, COLS + h * HEAD : COLS + (h + 1) * HEAD] = tn(d_s, q).astype(bf16)
            dp_ref[rows, 2 * COLS + h * HEAD : 2 * COLS + (h + 1) * HEAD] = tn(p.astype(bf16), d_o).astype(bf16)

    @pl.when(pl.program_id(0) >= HALF_STEPS)
    def _():
        sent_ref[...] = dp_ref[...]


def grads_kernel(count, where_ref, xa_ref, xb_ref, ca_ref, cb_ref, dp_ref, att_ref, _, *refs):
    step = pl.program_id(0)
    core, xl = where_ref[count], where_ref[count + 1]
    g_refs, (x_ref, cot_ref) = refs[: 2 * count], refs[2 * count :]
    x_ref[:PART, :], x_ref[PART:, :] = xa_ref[...], xb_ref[...]
    cot_ref[:PART, :], cot_ref[PART:, :] = ca_ref[...], cb_ref[...]
    gq = tn(x_ref[...], dp_ref[...]).astype(bf16)
    go = tn(cot_ref[...], att_ref[...]).astype(bf16)
    for n in range(count):
        for t in range(2):

            @pl.when(jnp.logical_and(step == n, xl == t))
            def _():
                for part in range(4):
                    g_ref = g_refs[2 * n + ((part // 2) ^ t)]
                    rows = slice(part * BLK, (part + 1) * BLK)
                    place = (part % 2) ^ core
                    for blk in range(2):
                        for i in range(3):
                            g_ref[place, blk, i] = gq[rows, (2 * i + blk) * BLK : (2 * i + blk + 1) * BLK]
                        g_ref[place, blk, 3] = go[rows, blk * BLK : (blk + 1) * BLK]


def product(lead, out, pair, slots):
    for n, (ref, at) in enumerate(slots):
        target = pair if ref else lead
        target[at * WIN : (at + 1) * WIN, :] = out[n * WIN : (n + 1) * WIN, :]


def rolled_kernel(dp_ref, in_ref, w_ref, other_ref, x_ref, _, lead_ref, pair_ref, gain_ref):
    total = nt(dp_ref[...], w_ref[...]) + nt(in_ref[...], other_ref[...])
    product(lead_ref, total.astype(bf16), pair_ref, ((0, 0), (0, 1), (1, 0), (1, 1)))
    gain_ref[...] = jnp.sum(total * x_ref[...].astype(f32), 0, keepdims=True)


def branch_kernel(att_ref, w_ref, _, own_ref, sib_ref):
    total = nt(att_ref[...], w_ref[...]).astype(bf16)
    own_ref[...] = total[:PART]
    sib_ref[...] = total[PART:]


def finish_kernel(where_ref, a_ref, b_ref, c_ref, d_ref, gq_ref, go_ref):
    for n, ref in enumerate((a_ref, b_ref, c_ref, d_ref)):
        rows = pl.ds(pl.multiple_of(where_ref[4 + n] * BLK, BLK), BLK)
        for i in range(3):
            gq_ref[i, rows, :] = ref[0, i].astype(f32)
        go_ref[:, rows] = ref[0, 3].astype(f32).T


def params():
    return pltpu.CompilerParams(dimension_semantics=("arbitrary",), vmem_limit_bytes=63 * 1024 * 1024)


PART = TOK // 2
HALF_STEPS = SLOTS // STEP // 2
own_spec = pl.BlockSpec((ROWS, D), lambda i: (jnp.minimum(i, HALF_STEPS - 1), 0))
sib_spec = pl.BlockSpec((ROWS, D), lambda i: (jnp.maximum(i - HALF_STEPS, 0), 0))
p_spec = pl.BlockSpec((STEP, HEADS_DEV, WIN, WIN), lambda i: (i, 0, 0, 0))
smem = pl.BlockSpec(memory_space=pltpu.SMEM)
unread = pl.BlockSpec(memory_space=pl.ANY)
WIDE, STRIP = 1024, 512
strip_column = pl.BlockSpec((PART, STRIP), lambda i: (0, i))
wide_column = pl.BlockSpec((PART, WIDE), lambda i: (0, i))


def rows_spec(cols):
    return pl.BlockSpec((ROWS, cols), lambda i: (i, 0))


def later_spec(cols):
    return pl.BlockSpec((ROWS, cols), lambda i: (jnp.maximum(i - HALF_STEPS, 0), 0))


def whole(*shape):
    return pl.BlockSpec(shape, lambda *i: (0,) * len(shape))


def shaped(shape, dtype=bf16):
    return jax.ShapeDtypeStruct(shape, dtype)


def forward(cut, pos, own, sib, weights):
    return pl.pallas_call(
        forward_kernel,
        grid=(SLOTS // STEP,),
        in_specs=[smem, smem, own_spec, sib_spec] + [whole(*w.shape) for w in weights],
        out_specs=[
            rows_spec(3 * COLS),
            rows_spec(COLS),
            p_spec,
            whole(D, 3 * COLS),
            whole(D, COLS),
        ],
        out_shape=[
            shaped((TOK, 3 * COLS)),
            shaped((TOK, COLS)),
            shaped((SLOTS, HEADS_DEV, WIN, WIN), f32),
            shaped((D, 3 * COLS)),
            shaped((D, COLS)),
        ],
        scratch_shapes=[pltpu.VMEM((ROWS, D), bf16)],
        compiler_params=params(),
        name="attention_forward",
    )(cut, pos, own, sib, *weights)


def backward(own, sib, qkv, p, wo, before):
    return pl.pallas_call(
        backward_kernel,
        grid=(SLOTS // STEP,),
        in_specs=[own_spec, sib_spec, rows_spec(3 * COLS), p_spec, whole(D, COLS), unread],
        out_specs=[rows_spec(3 * COLS), later_spec(3 * COLS)],
        out_shape=[shaped((TOK, 3 * COLS)), shaped((PART, 3 * COLS))],
        scratch_shapes=[pltpu.VMEM((ROWS, D), bf16)],
        compiler_params=params(),
        name="attention_backward",
    )(own, sib, qkv, p, wo, before)


def grads(lats, xl, core, xs, cots, dp, att, before):
    count = len(lats)
    part = pl.BlockSpec((PART, 4 * BLK), lambda i, where: (0, where[i]))
    return pl.pallas_call(
        functools.partial(grads_kernel, count),
        grid_spec=pltpu.PrefetchScalarGridSpec(
            num_scalar_prefetch=1,
            grid=(count,),
            in_specs=[part] * 4 + [whole(TOK, 3 * COLS), whole(TOK, COLS), unread],
            out_specs=[whole(2, 2, 4, BLK, BLK)] * (2 * count),
            scratch_shapes=[pltpu.VMEM((TOK, 4 * BLK), bf16)] * 2,
        ),
        out_shape=[shaped((2, 2, 4, BLK, BLK))] * (2 * count),
        compiler_params=params(),
        name="weight_gradients",
    )(jnp.stack(list(lats) + [core, xl]), *xs, *cots, dp, att, before)


def rolled_gradient(dp, dp_in, wq, wq_in, x, before):
    depth = 3 * COLS
    strip = pl.BlockSpec((STRIP, depth), lambda i: (i, 0))
    half = pl.BlockSpec((PART // 2, STRIP), lambda i: (0, i))
    return pl.pallas_call(
        rolled_kernel,
        grid=(D // STRIP,),
        in_specs=[whole(PART, depth)] * 2 + [strip] * 2 + [strip_column, unread],
        out_specs=[half, half, pl.BlockSpec((1, STRIP), lambda i: (0, i))],
        out_shape=[shaped((PART // 2, D))] * 2 + [shaped((1, D), f32)],
        compiler_params=params(),
        name="rolled_gradient",
    )(dp, dp_in, wq, wq_in, x, before)


def branch_product(att, wo, before):
    return pl.pallas_call(
        branch_kernel,
        grid=(D // WIDE,),
        in_specs=[whole(TOK, COLS), pl.BlockSpec((WIDE, COLS), lambda i: (i, 0)), unread],
        out_specs=[wide_column, wide_column],
        out_shape=[shaped((PART, D))] * 2,
        compiler_params=params(),
        name="branch_product",
    )(att, wo, before)


def finish(where, parts):
    return pl.pallas_call(
        finish_kernel,
        grid_spec=pltpu.PrefetchScalarGridSpec(
            num_scalar_prefetch=1,
            grid=(4,),
            in_specs=[pl.BlockSpec((1, 4, BLK, BLK), lambda s, where: (s, 0, 0, 0))] * 4,
            out_specs=[
                pl.BlockSpec((3, 4 * BLK, BLK), lambda s, where: (0, where[s], 0)),
                pl.BlockSpec((BLK, 4 * BLK), lambda s, where: (0, where[s])),
            ],
        ),
        out_shape=[shaped((3, D, BLK), f32), shaped((BLK, D), f32)],
        compiler_params=params(),
        name="finish_gradients",
    )(where, *parts)


def small(body, ins, outs, before=(), specs=(), scratch=(), name=None):
    specs = dict(specs)
    in_specs = [specs.get(n, whole(*x.shape)) for n, x in enumerate(ins)] + [unread] * len(before)
    count, extra = len(ins), len(before)

    def kernel(*refs):
        body(*refs[:count], *refs[count + extra :])

    return pl.pallas_call(
        kernel,
        grid=(1,),
        in_specs=in_specs,
        out_specs=[whole(*x.shape) for x in outs],
        out_shape=list(outs),
        scratch_shapes=list(scratch),
        compiler_params=params(),
        name=name,
    )(*ins, *before)


QUARTER = WIN // 4
UNIT = (4, BLK, BLK)
PAIR = (2,) + UNIT
FOUR = (2, 2) + UNIT
GAIN = (16, BLK)


def wide(*refs):
    total = refs[0].astype(f32)
    for ref in refs[1:]:
        total = total + ref.astype(f32)
    return total


def add_low(*values):
    return wide(*values).astype(bf16)


def select_body(half_ref, u0, u1, u2, u3, keep, give):
    @pl.when(half_ref[0] == 0)
    def _():
        keep[0], keep[1], give[0], give[1] = u0[...], u1[...], u2[...], u3[...]

    @pl.when(half_ref[0] != 0)
    def _():
        keep[0], keep[1], give[0], give[1] = u2[...], u3[...], u0[...], u1[...]


def join_body(*refs):
    out = refs[-1]
    for n, ref in enumerate(refs[:-1]):
        out[n] = ref[...]


def rows_body(*refs):
    out = refs[-1]
    for n, ref in enumerate(refs[:-1]):
        out[n * WIN : (n + 1) * WIN, :] = ref[...]


def pin_body(out):
    out[...] = jnp.zeros_like(out)


def normal(values):
    centered = values - jnp.mean(values, -1, keepdims=True)
    inverse_std = lax.rsqrt(jnp.mean(centered * centered, -1, keepdims=True) + EPSILON)
    return centered * inverse_std, inverse_std


def enter_body(own, right, below, corner, gain, rolled, cot, normed, buffer):
    for n, out in enumerate((rolled, cot)):
        for k, piece in enumerate((own, right, below, corner)):
            buffer[k * QUARTER : (k + 1) * QUARTER, :] = piece[n].astype(f32)
        out[...] = buffer[...].astype(bf16)
        if n == 0:
            normed[...] = (normal(buffer[...])[0] * gain[...]).astype(bf16)


def leave_body(rolled, cot, gain, b0, b1, b2, d0, d1, d2, own, right, below, corner, buffer):
    branch = add_low(b0[...], b1[...], b2[...])
    buffer[...] = rolled[...].astype(f32) + branch.astype(f32)
    for k, piece in enumerate((own, right, below, corner)):
        piece[0] = buffer[k * QUARTER : (k + 1) * QUARTER, :].astype(bf16)
    standard, inverse_std = normal(rolled[...].astype(f32))
    scaled = add_low(d0[...], d1[...], d2[...]).astype(f32) * gain[...]
    local = inverse_std * (
        scaled
        - jnp.mean(scaled, -1, keepdims=True)
        - standard * jnp.mean(scaled * standard, -1, keepdims=True)
    )
    buffer[...] = cot[...].astype(f32) + local
    for k, piece in enumerate((own, right, below, corner)):
        piece[1] = buffer[k * QUARTER : (k + 1) * QUARTER, :].astype(bf16)


def windows_body(own, other, lead, pair):
    for n, (out, at) in enumerate(((lead, 0), (pair, 0), (lead, 1), (pair, 1))):
        rows = slice(n * WIN, (n + 1) * WIN)
        out[at * WIN : (at + 1) * WIN, :] = add_low(own[rows, :], other[rows, :])


def mid_body(lead, given, out):
    out[...] = add_low(lead[...], given[...])


def gain_mid_body(lead, given, gain, gain_in, out, gain_out):
    mid_body(lead, given, out)
    gain_out[...] = gain[...] + gain_in[...]


def sides_body(g10, g11, g30, g31, back1, back3, to1, to3):
    to1[0], to1[1] = g10[...], add_low(g11[...], back1[...])
    to3[0], to3[1] = add_low(g30[...], back3[...]), g31[...]


def lat_body(g00, g01, in1, in3, gain, gain_in, t0, t1, gain_out):
    t0[...] = add_low(g00[...], in1[0], in3[0])
    t1[...] = add_low(g01[...], in1[1], in3[1])
    gain_out[...] = gain[...] + gain_in[...]


def xl_body(t0, crossing, gain, gain_in, ours, others, gain_out):
    ours[...] = add_low(t0[0], crossing[0])
    others[...] = add_low(t0[1], crossing[1])
    gain_out[...] = gain[...] + gain_in[...]


def core_body(half_ref, ours, theirs, gain, gain_in, s0, s1, s2, s3, gain_out):
    gain_out[...] = gain[...] + gain_in[...]

    @pl.when(half_ref[0] == 0)
    def _():
        s0[...], s1[...], s2[...], s3[...] = ours[0], ours[1], theirs[0], theirs[1]

    @pl.when(half_ref[0] != 0)
    def _():
        s0[...], s1[...], s2[...], s3[...] = theirs[0], theirs[1], ours[0], ours[1]


def gain_body(gain, gain_in, gain_out):
    gain_out[...] = gain[...] + gain_in[...]


def zh_body(kept, b1, b2, b3, gain, gain_in, unit, gain_out):
    unit[...] = add_low(kept[...], b1[...], b2[...], b3[...])
    gain_out[...] = gain[...] + gain_in[...]


def rows_gain_body(u0, u1, u2, u3, gain, gain_in, rows, gain_out):
    rows[0], rows[1], rows[2], rows[3] = u0[...], u1[...], u2[...], u3[...]
    gain_out[...] = gain[...] + gain_in[...]


def shift(x, axes, by):
    count = lax.axis_size(axes)
    return lax.ppermute(x, axes, [(i, (i + by) % count) for i in range(count)])


def swap(x, axes, mask):
    count = lax.axis_size(axes)
    return lax.ppermute(x, axes, [(i, i ^ mask) for i in range(count)])


def shift_both(x, by):
    rows, cols = lax.axis_size(ROW), lax.axis_size(LON)
    pairs = [
        (r * cols + c, (r + by) % rows * cols + (c + by) % cols)
        for r in range(rows)
        for c in range(cols)
    ]
    return lax.ppermute(x, ALL, pairs)


def quarters(*arrays):
    arrays = [x.transpose(0, 2, 1, 3) for x in arrays]
    lon = WLON // 2

    def cut(rows, cols):
        return jnp.stack([x[rows, cols].reshape(QUARTER, D) for x in arrays])

    first, last = slice(0, CLAT), slice(CLAT, 2 * CLAT)
    west, east = slice(0, lon), slice(lon, WLON)
    below = shift(cut(first, east), ROW, -1)
    corner = shift_both(cut(first, west), -1)
    right = shift(cut(last, west), LON, -1)
    return cut(last, east), right, below, corner


def back_home(before, own, right, below, corner):
    below, corner, right = shift(below, ROW, 1), shift_both(corner, 1), shift(right, LON, 1)
    below, corner, right, _ = lax.optimization_barrier((below, corner, right, before))
    results = []
    for n in range(2):
        o, r, b, c = (x[n].reshape(CLAT, WLON // 2, LEV, D) for x in (own, right, below, corner))
        top = jnp.concatenate([c, b], axis=1)
        bottom = jnp.concatenate([r, o], axis=1)
        results.append(jnp.concatenate([top, bottom], axis=0).transpose(0, 2, 1, 3))
    return results


def weight_unit(w_qkv, w_out, place):
    qkv = lax.dynamic_slice(w_qkv.transpose(1, 0, 2), (0, place * BLK, 0), (3, BLK, BLK))
    out = lax.dynamic_slice(w_out, (0, place * BLK), (BLK, BLK)).T
    return jnp.concatenate([qkv, out[None]], axis=0)


def shards(tokens, norm_gain, w_qkv, w_out, grad_out):
    zh, lat, xl, core = (lax.axis_index(a) for a in ("zh", "lat", "xl", "core"))
    half = ((zh // 2) ^ core).reshape(1)
    chips = {(s, t): (lat ^ s) * 2 + (xl ^ t) for s in range(4) for t in range(2)}
    pos = jnp.stack([chips[place] * 2 + (core ^ c) for place in sorted(chips) for c in range(2)])
    ends = jnp.stack(
        [lat ^ s for s in range(4)] + [(xl ^ t) * 2 + (core ^ c) for c in range(2) for t in range(2)]
    )
    edge = jnp.logical_and(zh == 3, lat == 3)
    owners = lax.axis_index(NEAR) ^ (jnp.arange(SLOTS) % 4)
    cut = jnp.logical_and(edge, owners == 3).astype(jnp.int32)
    gain_row = norm_gain.reshape(1, D)
    token = shaped((8, BLK), f32)
    window, windows = shaped((WIN, D)), shaped((4 * WIN, D))
    scalar = {0: smem}

    unit = weight_unit(w_qkv, w_out, pos[0])
    units = [unit] + [swap(unit, "zh", s) for s in (1, 2, 3)]
    pieces = quarters(tokens, grad_out)
    keep, give = small(select_body, [half] + units, [shaped(PAIR)] * 2, specs=scalar, name="select")
    given = swap(give, "core", 1)
    buffer = [pltpu.VMEM((WIN, D), f32)]
    rolled, cotangent, normed = small(
        enter_body, [*pieces, gain_row], [window] * 3, before=[give], scratch=buffer, name="enter"
    )
    (mine,) = small(join_body, [keep, given], [shaped(FOUR)], before=[normed], name="join")
    near = swap(mine, "xl", 1)
    m1a, m3a = swap(mine, "lat", 1), swap(mine, "lat", 3)
    x1, x2 = swap(normed, NEAR, 1), swap(normed, NEAR, 2)
    (pin,) = small(pin_body, [], [token], before=[near, m1a, m3a], name="pin")
    m1b, m3b = swap(near, "lat", 1), swap(near, "lat", 3)
    o0 = swap(m1a, "lat", 3)
    (pin,) = small(pin_body, [], [token], before=[m1b, m3b, x1, x2, pin], name="pin")
    o1 = swap(m3b, "lat", 1)
    x3 = swap(lax.optimization_barrier((x1, pin))[0], NEAR, 2)
    (x_own,) = small(rows_body, [normed, x1, x2, x3], [windows], before=[o0, o1, pin], name="rows")
    x_sib = swap(x_own, "core", 1)
    c1, c2, c3 = (swap(cotangent, NEAR, s) for s in (1, 2, 3))

    weights = [mine, near, m1a, m1b, o0, o1, m3a, m3b]
    qkv, att, p, wq, wo = forward(cut, pos, x_own, x_sib, weights)
    (c_own,) = small(rows_body, [cotangent, c1, c2, c3], [windows], before=[wo], name="rows")
    c_sib = swap(c_own, "core", 1)
    b_own, b_sib = branch_product(att, wo, c_own)
    b_other = swap(b_sib, "core", 1)
    wq_in = swap(lax.optimization_barrier((wq, b_own))[0], "core", 1)
    dp, dp_sent = backward(c_own, c_sib, qkv, p, wo, b_own)
    dp_in = swap(dp_sent, "core", 1)
    xs, cots = (x_own, x_sib), (c_own, c_sib)

    far0, far1 = grads([lat ^ 2], xl, core, xs, cots, dp, att, dp)
    back3, back1 = swap(far0, "lat", 1), swap(far1, "lat", 3)
    near_lats = [lat ^ s for s in (1, 3, 0)]
    g10, g11, g30, g31, g00, g01 = grads(near_lats, xl, core, xs, cots, dp, att, far0)
    to1, to3 = small(
        sides_body, [g10, g11, g30, g31, back1, back3], [shaped((2,) + FOUR)] * 2, name="sides"
    )
    in1, in3 = swap(to1, "lat", 1), swap(to3, "lat", 3)
    first, second = pl.BlockSpec((WIN, D), lambda i: (0, 0)), pl.BlockSpec((WIN, D), lambda i: (1, 0))
    pair = shaped((2 * WIN, D))
    b_lead, b_pair = small(windows_body, [b_own, b_other], [pair] * 2, before=[to1], name="windows")
    b_in = swap(b_pair, NEAR, 1)
    d_lead, d_pair, gain = rolled_gradient(dp, dp_in, wq, wq_in, x_own, b_pair)
    d_in = swap(d_pair, NEAR, 2)

    gain, gain_shape = gain.reshape(GAIN), shaped(GAIN, f32)
    gain_in = swap(gain, ALL, 1)
    (gain,) = small(gain_body, [gain, gain_in], [gain_shape], before=[d_pair], name="gain")
    gain_in = swap(gain, ALL, 4)
    t0, t1, gain = small(
        lat_body,
        [g00, g01, in1, in3, gain, gain_in],
        [shaped(FOUR), shaped(FOUR), gain_shape],
        name="lat_sum",
    )
    crossing, gain_in = swap(t1, "xl", 1), swap(gain, ALL, 8)
    b_mid, gain = small(
        gain_mid_body,
        [b_lead, b_in, gain, gain_in],
        [window, gain_shape],
        before=[t1],
        specs={0: second, 1: second},
        name="mid",
    )
    b_last, gain_in = swap(b_mid, NEAR, 2), swap(gain, ALL, 2)
    ours, others, gain = small(
        xl_body,
        [t0, crossing, gain, gain_in],
        [shaped(PAIR)] * 2 + [gain_shape],
        before=[b_mid],
        name="xl_sum",
    )
    theirs, gain_in = swap(others, "core", 1), swap(gain, ALL, 32)
    (d_mid,) = small(
        mid_body, [d_lead, d_in], [window], before=[ours], specs={0: second, 1: second}, name="mid"
    )
    d_last = swap(d_mid, NEAR, 1)
    *sent, gain = small(
        core_body,
        [half, ours, theirs, gain, gain_in],
        [shaped(UNIT)] * 4 + [gain_shape],
        before=[d_mid, b_last],
        specs=scalar,
        name="core_sum",
    )
    back = [swap(sent[s], "zh", s) for s in (1, 2, 3)]
    gain_in = swap(gain, ALL, 16)
    (gain,) = small(gain_body, [gain, gain_in], [gain_shape], before=[sent[1], d_last], name="gain")
    gain_in = swap(gain, ALL, 64)
    unit, gain = small(
        zh_body, [sent[0], *back, gain, gain_in], [shaped(UNIT), gain_shape], name="zh_sum"
    )
    around, gain_in = [swap(unit, "lat", s) for s in (1, 2, 3)], swap(gain, ALL, 128)
    results = small(
        leave_body,
        [rolled, cotangent, gain_row, b_lead, b_in, b_last, d_lead, d_in, d_last],
        [shaped((2, QUARTER, D))] * 4,
        before=[unit],
        specs={n: first for n in (3, 4, 6, 7)},
        scratch=buffer,
        name="leave",
    )
    rows, gain = small(
        rows_gain_body,
        [unit, *around, gain, gain_in],
        [shaped((4,) + UNIT), gain_shape],
        before=[results[0]],
        name="slices",
    )
    near_rows, core_rows = swap(rows, "xl", 1), swap(rows, "core", 1)
    results, _ = lax.optimization_barrier((results, rows))
    output, grad_tokens = back_home(rows, *results)
    near_rows, output, _ = lax.optimization_barrier((near_rows, output, grad_tokens))
    last_rows = swap(near_rows, "core", 1)
    grad_wqkv, grad_wout = finish(ends, [rows, near_rows, core_rows, last_rows])
    grad_gain = gain.reshape(D) / norm_gain
    return output, grad_tokens, grad_wqkv.transpose(1, 0, 2), grad_wout, grad_gain


def solution(mesh):
    fine = Mesh(mesh.devices.reshape(4, 2, 2, 4, 2, 2), ALL)
    by_token = P(ROW, None, LON, None)
    in_specs = (by_token, P(), P(None, None, OUTER), P(OUTER, None), by_token)
    out_specs = (by_token, by_token, P(None, None, OUTER), P(OUTER, None), P())
    return jax.shard_map(shards, mesh=fine, in_specs=in_specs, out_specs=out_specs, check_vma=False)
```
